512 devices in a mesh: seq: 64 (over x, z), exp: 8 (over y, core).
Axes of the slice: x: 4, y: 4, z: 16, core: 2. Of those that a mesh axis runs over, the one named last changes fastest.
Arguments:
- tokens: bfloat16 [16384, 6144], P('seq', 'exp'), may hold values from -24 to 24
- slot_param: bfloat16 [256, 6144], P('exp', 'seq'), may hold values from -4 to 4
- slot_outputs: bfloat16 [256, 6144], P('exp', 'seq'), may hold values from -6 to 6
- grad_output: bfloat16 [16384, 6144], P('seq', 'exp'), may hold values from -6 to 6
- grad_slot_in: bfloat16 [256, 6144], P('exp', 'seq'), may hold values from -6 to 6
Outputs:
- slot_inputs: bfloat16 [256, 6144], P('exp', 'seq')
- layer_output: bfloat16 [16384, 6144], P('seq', 'exp')
- grad_tokens: bfloat16 [16384, 6144], P('seq', 'exp')
- grad_param: bfloat16 [256, 6144], P('exp', 'seq')
- grad_slot_out: bfloat16 [256, 6144], P('exp', 'seq')
The draws below stay inside these ranges and needn't reach their ends.
All inputs are finite; a program needn't handle non-finite values.
Results may differ from the reference program's by a relative error of at most 0.0057.
Values may be sent and summed in bfloat16 or wider, within the bound.
A program may use at most 64 MiB of HBM per device.

```python
import math
import jax
import jax.numpy as jnp

D = 6144
SLOTS = 256
TOKENS = 16384


twin_pairs = 3


param_lift = 8.0


def shared_base(key):
    return jax.random.normal(key, (SLOTS, D), jnp.float32)


def draw_slot_param(key, part):
    base_rows = shared_base(key)
    key = jax.random.fold_in(key, 11)
    scale_key, twin_key = jax.random.split(key)
    row_index = jnp.arange(SLOTS)[:, None]
    column_scale = jnp.exp(jax.random.uniform(scale_key, (SLOTS, 1), jnp.float32, math.log(0.3), math.log(3.0)))
    aligned = row_index < 2 * twin_pairs
    column_scale = jnp.where(aligned, param_lift, column_scale)
    shifted = jnp.roll(base_rows, 1, axis=0) + 0.6 * jax.random.normal(twin_key, (SLOTS, D), jnp.float32)
    twin_rows = (row_index % 2 == 1) & aligned
    base_rows = jnp.where(twin_rows, shifted, base_rows)
    return jnp.clip(base_rows * column_scale / math.sqrt(D), -4.0, 4.0).astype(jnp.bfloat16)


def draw_tokens(key, part):
    base_rows = shared_base(key)
    key = jax.random.fold_in(key, 12)
    scale_key = jax.random.fold_in(key, 0)
    value_key = jax.random.fold_in(key, 1)
    extra_key = jax.random.fold_in(key, 3)
    row_scale = jnp.exp(jax.random.uniform(scale_key, (TOKENS, 1), jnp.float32, math.log(0.3), math.log(3.0)))
    values = jax.random.normal(value_key, (TOKENS, D), jnp.float32) * row_scale
    aligned_slots = 2 * (jnp.arange(2 * twin_pairs) // 2)
    gain_values = jnp.array([1.5, 1.53, 3.0, 3.03, 4.5, 4.53], jnp.float32)
    positions = jnp.arange(2 * twin_pairs) * (TOKENS // (2 * twin_pairs)) + 3
    token_lift = gain_values[:, None] * (100.0 / param_lift) / math.sqrt(D)
    planted = token_lift * (base_rows[aligned_slots] + 0.3 * jax.random.normal(extra_key, (2 * twin_pairs, D), jnp.float32))
    values = values.at[positions].set(planted)
    return jnp.clip(values, -24.0, 24.0).astype(jnp.bfloat16)


def block_levels(rng, dims, cuts, low, high):
    factor_of = 1.0
    for position, shards_of in cuts:
        steps = jax.random.uniform(jax.random.fold_in(jax.random.fold_in(rng, 6), position), (shards_of,), jnp.float32, low / len(cuts), high / len(cuts))
        factor_of = factor_of * jnp.repeat(jnp.exp(steps), dims[position] // shards_of).reshape((-1,) + (1,) * (len(dims) - 1 - position))
    return factor_of


def normal_values(own_key, shape, spread, reach, cuts=(), dtype=jnp.bfloat16):
    loudness = block_levels(own_key, shape, cuts, -0.22, 0.18) if cuts else 1.0
    result = jax.random.normal(own_key, shape, jnp.float32) * spread * loudness
    return jnp.minimum(jnp.maximum(result, -reach), reach).astype(dtype)


def setup_inputs(seed: int = 0) -> dict:
    splits = jax.random.split(jax.random.key(seed), 6)
    tokens = draw_tokens(jax.random.fold_in(splits[5], 71), 0)
    slot_param = draw_slot_param(jax.random.fold_in(splits[5], 71), 0)
    slot_outputs = normal_values(splits[2], (SLOTS, D), 1.0, 6.0, ((0, 8), (1, 64)))
    grad_output = normal_values(splits[3], (TOKENS, D), 1.0, 6.0, ((0, 64), (1, 8)))
    grad_slot_in = normal_values(splits[4], (SLOTS, D), 1.0, 6.0, ((0, 8), (1, 64)))
    return dict(tokens=tokens, slot_param=slot_param, slot_outputs=slot_outputs, grad_output=grad_output, grad_slot_in=grad_slot_in)


def reference(tokens, slot_param, slot_outputs, grad_output, grad_slot_in):
    logits = jnp.dot(tokens, slot_param.T, preferred_element_type=jnp.float32)
    col_max = jnp.max(logits, axis=0)
    col_total = jnp.sum(jnp.exp(logits - col_max), axis=0)
    dispatch_full = jnp.exp(logits - col_max) / col_total
    dispatch = dispatch_full.astype(jnp.bfloat16)
    row_max = jnp.max(logits, axis=1, keepdims=True)
    row_weights = jnp.exp(logits - row_max)
    combine_full = row_weights / jnp.sum(row_weights, axis=1, keepdims=True)
    combine = combine_full.astype(jnp.bfloat16)
    slot_inputs = jnp.dot(dispatch.T, tokens, preferred_element_type=jnp.float32).astype(jnp.bfloat16)
    layer_output = jnp.dot(combine, slot_outputs, preferred_element_type=jnp.float32).astype(jnp.bfloat16)
    grad_slot_out = jnp.dot(combine.T, grad_output, preferred_element_type=jnp.float32).astype(jnp.bfloat16)
    grad_combine = jnp.dot(grad_output, slot_outputs.T, preferred_element_type=jnp.float32)
    grad_dispatch = jnp.dot(tokens, grad_slot_in.T, preferred_element_type=jnp.float32)
    from_combine = combine_full * (grad_combine - jnp.sum(combine_full * grad_combine, axis=1, keepdims=True))
    from_dispatch = dispatch_full * (grad_dispatch - jnp.sum(dispatch_full * grad_dispatch, axis=0))
    grad_logits = (from_combine + from_dispatch).astype(jnp.bfloat16)
    grad_tokens = (jnp.dot(dispatch, grad_slot_in, preferred_element_type=jnp.float32)
                   + jnp.dot(grad_logits, slot_param, preferred_element_type=jnp.float32)).astype(jnp.bfloat16)
    grad_param = jnp.dot(grad_logits.T, tokens, preferred_element_type=jnp.float32).astype(jnp.bfloat16)
    return slot_inputs, layer_output, grad_tokens, grad_param, grad_slot_out
```

```python
import functools

import jax
import jax.numpy as jnp
from jax import lax
from jax.experimental import pallas as pl
from jax.experimental.pallas import tpu as pltpu
from jax.sharding import PartitionSpec as P

MESH = pl.DeviceIdType.MESH
F32 = jnp.float32
BF16 = jnp.bfloat16

NEAR = [(dx, dz) for dz in (2, 1, -1, 0) for dx in (2, 1, 3, 0) if (dx, dz) != (0, 0)]
FAR = [8, 4, -4]
GROUP = [(dy, dc) for dy in (2, 1, 3, 0) for dc in (1, 0) if (dy, dc) != (0, 0)]
PARAM, COTAN, OUTPUT = 0, 1, 2
BACK, SLOT, GPARAM = 0, 1, 2


def rows_by_rows(left, right):
    return lax.dot_general(left, right, (((1,), (1,)), ((), ())), preferred_element_type=F32)


def columns_by_columns(left, right):
    return lax.dot_general(left, right, (((0,), (0,)), ((), ())), preferred_element_type=F32)


def dot(left, right):
    return jnp.dot(left, right, preferred_element_type=F32)


def kernel(
    tok_ref, par_ref, out_ref, go_ref, gsi_ref,
    slot_in_ref, layer_ref, gtok_ref, gpar_ref, gso_ref,
    blk, w, tp, gp, part, red, mine, full, st_m, st_u, far_m, far_u, comb, q, r1, hold, coll,
    sp_s, sp_r, ag_s, ag_r, rs_s, rs_r, eg_s, eg_r, nm_s, nm_r, fm_s, fm_r, p1_s, p1_r, p2_s, p2_r,
):
    s, e = lax.axis_index("seq"), lax.axis_index("exp")
    x, z = s // 16, s % 16
    y, c = e // 2, e % 2
    k = z % 4
    two = 2 - 4 * c

    def near_of(dx, dz):
        dz = two if dz == 2 else dz
        return (x + dx) % 4, (z + dz + 16) % 16

    def near_id(dx, dz):
        nx, nz = near_of(dx, dz)
        return (nx * 16 + nz, e)

    def near_source(dx, dz):
        dz = two if dz == 2 else dz
        return (x - dx + 4) % 4, (z - dz + 16) % 16

    def far_id(dz):
        return (x * 16 + (z + dz + 16) % 16, e)

    def group_id(dy, dc):
        return (s, ((y + dy) % 4) * 2 + (c + dc) % 2)

    h_me = (z % 8) // 4

    def holder_id(g):
        return (y * 16 + (z + 4 * g) % 16, x * 2 + z // 8)

    own_self = (y == x) & (c == z // 8)

    def owner_id(h, cc):
        return (y * 16 + 8 * c + 4 * h + k, x * 2 + cc)

    def holder_g(h):
        return (z // 4 - 2 * c - h + 8) % 4

    def owner_is_self(h, cc):
        return (x == y) & (z == 8 * c + 4 * h + k) & (c == cc)

    barrier = pltpu.get_barrier_semaphore()

    def greet(device):
        pl.semaphore_signal(barrier, inc=1, device_id=device, device_id_type=MESH)

    for g in (2, 1, 3):
        greet(holder_id(g))

    @pl.when(jnp.logical_not(own_self))
    def _():
        greet(holder_id(0))

    for h in (0, 1):
        for cc in (0, 1):
            @pl.when(jnp.logical_not(owner_is_self(h, cc)))
            def _():
                greet(owner_id(h, cc))

    for dz in FAR:
        greet(far_id(dz))
    for o in NEAR:
        nx, nz = near_source(*o)
        greet((nx * 16 + nz, e))
    for o in GROUP:
        greet(group_id(*o))

    blk[...] = jnp.zeros_like(blk)
    blk[PARAM, :, 0:96] = par_ref[...]
    blk[COTAN, :, 0:96] = gsi_ref[...]
    blk[OUTPUT, :, 0:96] = out_ref[...]
    for src, dst in ((tok_ref, tp), (go_ref, gp)):
        dst[...] = jnp.zeros_like(dst)
        for j in range(8):
            j2 = 2 * (j % 4) + j // 4
            dst[:, 128 * j2:128 * j2 + 96] = src[:, 96 * j:96 * j + 96]

    pl.semaphore_wait(barrier, len(FAR) + len(NEAR) + len(GROUP) + 8 - 2 * own_self.astype(jnp.int32))

    sent = []

    def send(src, dst, ss, rs, device, unless=None):
        cp = pltpu.make_async_remote_copy(
            src_ref=src, dst_ref=dst, send_sem=ss, recv_sem=rs, device_id=device, device_id_type=MESH
        )
        if unless is None:
            cp.start()
        else:
            pl.when(jnp.logical_not(unless))(cp.start)
        sent.append((unless, cp))

    def receive(ref, ss, rs, unless=None):
        cp = pltpu.make_async_remote_copy(
            src_ref=ref, dst_ref=ref, send_sem=ss, recv_sem=rs, device_id=near_id(1, 0), device_id_type=MESH
        )
        if unless is None:
            cp.wait_recv()
        else:
            pl.when(jnp.logical_not(unless))(cp.wait_recv)

    own_row = pl.multiple_of(64 * y + 32 * c, 32)
    own_col = pl.multiple_of(128 * (2 * k + h_me), 128)
    for a in (PARAM, COTAN, OUTPUT):
        spot = w.at[a, pl.ds(own_row, 32), pl.ds(own_col, 128)]
        for g in (2, 1, 3):
            send(blk.at[a], spot, sp_s.at[a, g], sp_r.at[a, 2 * h_me + c], holder_id(g))
        send(blk.at[a], spot, sp_s.at[a, 0], sp_r.at[a, 2 * h_me + c], holder_id(0), own_self)

        @pl.when(own_self)
        def _():
            w[a, pl.ds(own_row, 32), pl.ds(own_col, 128)] = blk[a]

    held_row = pl.multiple_of(64 * x, 64)
    held_col = pl.multiple_of(256 * k, 256)
    for a in (PARAM, COTAN, OUTPUT):
        for h in (0, 1):
            for cc in (0, 1):
                spot = w.at[a, pl.ds(held_row + 32 * cc, 32), pl.ds(held_col + 128 * h, 128)]
                receive(spot, sp_s.at[a, 0], sp_r.at[a, 2 * h + cc], owner_is_self(h, cc))
        spot = w.at[a, pl.ds(held_row, 64), pl.ds(held_col, 256)]
        for i, o in enumerate(NEAR):
            send(spot, spot, ag_s.at[a, i], ag_r.at[a, i], near_id(*o))

    def gathered(a):
        for i, (dx, dz) in enumerate(NEAR):
            nx, nz = near_source(dx, dz)
            spot = w.at[
                a,
                pl.ds(pl.multiple_of(64 * nx, 64), 64),
                pl.ds(pl.multiple_of(256 * (nz % 4), 256), 256),
            ]
            receive(spot, ag_s.at[a, i], ag_r.at[a, i])

    def scatter(a):
        for i, o in enumerate(GROUP):
            device = group_id(*o)
            spot = part.at[a, pl.ds(pl.multiple_of(32 * device[1], 32), 32)]
            send(spot, red.at[a, i], rs_s.at[a, i], rs_r.at[a, i], device)

    my_tok = pl.multiple_of(32 * e, 32)

    def gather(a):
        total = part[a, pl.ds(my_tok, 32), :]
        for i in range(len(GROUP)):
            receive(red.at[a, i], rs_s.at[a, i], rs_r.at[a, i])
            total = total + red[a, i]
        mine[a] = total
        full[a, pl.ds(my_tok, 32), :] = total
        for i, o in enumerate(GROUP):
            send(mine.at[a], full.at[a, pl.ds(my_tok, 32)], eg_s.at[a, i], eg_r.at[a, i], group_id(*o))

    def complete(a):
        for i, (dy, dc) in enumerate(GROUP):
            ee = ((y - dy + 4) % 4) * 2 + (c + dc) % 2
            spot = full.at[a, pl.ds(pl.multiple_of(32 * ee, 32), 32)]
            receive(spot, eg_s.at[a, i], eg_r.at[a, i])

    gathered(PARAM)
    part[PARAM] = rows_by_rows(tp[...], w[PARAM])
    scatter(PARAM)
    gathered(COTAN)
    part[COTAN] = rows_by_rows(tp[...], w[COTAN])
    scatter(COTAN)
    gather(PARAM)
    gathered(OUTPUT)
    part[OUTPUT] = rows_by_rows(gp[...], w[OUTPUT])
    scatter(OUTPUT)
    gather(COTAN)
    complete(PARAM)

    logits = full[0]
    col_max = jnp.max(logits, axis=0, keepdims=True)
    expo = jnp.exp(logits - col_max)
    col_total = jnp.sum(expo, axis=0, keepdims=True)
    n = len(NEAR)
    st_m[n, 0:1] = col_max
    st_m[n, 1:2] = col_total
    for i, o in enumerate(NEAR):
        send(st_m.at[n], st_m.at[i], nm_s.at[0, i], nm_r.at[0, i], near_id(*o))

    row_max = jnp.max(logits, axis=1, keepdims=True)
    weights = jnp.exp(logits - row_max)
    combine_full = weights / jnp.sum(weights, axis=1, keepdims=True)
    comb[...] = combine_full
    combine = combine_full.astype(BF16)

    def partial(a, left, right_ref):
        left_t = left.T
        for kk in range(4):
            q[a, :, 256 * kk:256 * kk + 256] = dot(left_t, right_ref[:, 256 * kk:256 * kk + 256]).astype(BF16)
        for i, (dx, dz) in enumerate(NEAR):
            nx, nz = near_of(dx, dz)
            spot = q.at[
                a,
                pl.ds(pl.multiple_of(64 * nx, 64), 64),
                pl.ds(pl.multiple_of(256 * (nz % 4), 256), 256),
            ]
            send(spot, r1.at[a, i], p1_s.at[a, i], p1_r.at[a, i], near_id(dx, dz))

    def unpad(dst, j_value):
        for kk in range(4):
            value = j_value(kk).astype(BF16)
            for h in (0, 1):
                j = 4 * h + kk
                dst[:, 96 * j:96 * j + 96] = value[:, 128 * h:128 * h + 96]

    gather(OUTPUT)
    partial(BACK, combine, gp)

    complete(COTAN)
    expo = jnp.exp(full[0] - st_m[n, 0:1])
    st_u[n, 0:1] = jnp.sum(expo * full[COTAN], axis=0, keepdims=True)
    st_u[n, 1:2] = jnp.zeros((1, 256), F32)
    for i, o in enumerate(NEAR):
        send(st_u.at[n], st_u.at[i], nm_s.at[1, i], nm_r.at[1, i], near_id(*o))

    for i in range(n):
        receive(st_m.at[i], nm_s.at[0, i], nm_r.at[0, i])
    near_max = st_m[n, 0:1]
    for i in range(n):
        near_max = jnp.maximum(near_max, st_m[i, 0:1])
    near_total = jnp.zeros((1, 256), F32)
    factors = []
    for i in range(n + 1):
        factor = jnp.exp(st_m[i, 0:1] - near_max)
        factors.append(factor)
        near_total = near_total + factor * st_m[i, 1:2]
    far_m[3, 0:1] = near_max
    far_m[3, 1:2] = near_total
    for i, dz in enumerate(FAR):
        send(far_m.at[3], far_m.at[i], fm_s.at[0, i], fm_r.at[0, i], far_id(dz))

    for i in range(n):
        receive(st_u.at[i], nm_s.at[1, i], nm_r.at[1, i])
    near_inner = jnp.zeros((1, 256), F32)
    for i in range(n + 1):
        near_inner = near_inner + factors[i] * st_u[i, 0:1]
    far_u[3, 0:1] = near_inner
    far_u[3, 1:2] = jnp.zeros((1, 256), F32)
    for i, dz in enumerate(FAR):
        send(far_u.at[3], far_u.at[i], fm_s.at[1, i], fm_r.at[1, i], far_id(dz))

    complete(OUTPUT)
    unpad(layer_ref, lambda kk: dot(comb[...].astype(BF16), w[OUTPUT, :, 256 * kk:256 * kk + 256]))

    for i in range(3):
        receive(far_m.at[i], fm_s.at[0, i], fm_r.at[0, i])
    col_max = jnp.maximum(
        jnp.maximum(far_m[0, 0:1], far_m[1, 0:1]), jnp.maximum(far_m[2, 0:1], far_m[3, 0:1])
    )
    col_total = jnp.zeros((1, 256), F32)
    factors = []
    for i in range(4):
        factor = jnp.exp(far_m[i, 0:1] - col_max)
        factors.append(factor)
        col_total = col_total + factor * far_m[i, 1:2]
    dispatch_full = jnp.exp(full[0] - col_max) / col_total
    dispatch = dispatch_full.astype(BF16)
    partial(SLOT, dispatch, tp)

    for i in range(3):
        receive(far_u.at[i], fm_s.at[1, i], fm_r.at[1, i])
    inner = jnp.zeros((1, 256), F32)
    for i in range(4):
        inner = inner + factors[i] * far_u[i, 0:1]
    inner = inner / col_total
    combine_full = comb[...]
    grad_combine = full[OUTPUT]
    from_combine = combine_full * (
        grad_combine - jnp.sum(combine_full * grad_combine, axis=1, keepdims=True)
    )
    from_dispatch = dispatch_full * (full[COTAN] - inner)
    grad_logits = (from_combine + from_dispatch).astype(BF16)
    partial(GPARAM, grad_logits, tp)

    def to_owners(a):
        mx = pl.multiple_of(64 * x, 64)
        mk = pl.multiple_of(256 * k, 256)
        total = q[a, pl.ds(mx, 64), pl.ds(mk, 256)].astype(F32)
        for i in range(n):
            receive(r1.at[a, i], p1_s.at[a, i], p1_r.at[a, i])
            total = total + r1[a, i].astype(F32)
        total = total.astype(BF16)
        for h in (0, 1):
            for cc in (0, 1):
                hold[a, 2 * h + cc] = total[32 * cc:32 * cc + 32, 128 * h:128 * h + 128]
        for h in (0, 1):
            for cc in (0, 1):
                i = 2 * h + cc
                here = owner_is_self(h, cc)
                g = holder_g(h)
                send(hold.at[a, i], coll.at[a, g], p2_s.at[a, i], p2_r.at[a, g], owner_id(h, cc), here)

                @pl.when(here)
                def _():
                    coll[a, g] = hold[a, i]

    to_owners(BACK)
    to_owners(SLOT)
    unpad(
        gtok_ref,
        lambda kk: dot(dispatch, w[COTAN, :, 256 * kk:256 * kk + 256])
        + dot(grad_logits, w[PARAM, :, 256 * kk:256 * kk + 256]),
    )
    to_owners(GPARAM)

    for a, ref in ((BACK, gso_ref), (SLOT, slot_in_ref), (GPARAM, gpar_ref)):
        for g in range(4):
            receive(coll.at[a, g], p2_s.at[a, 0], p2_r.at[a, g], own_self if g == 0 else None)
        total = coll[a, 0].astype(F32)
        for g in range(1, 4):
            total = total + coll[a, g].astype(F32)
        ref[...] = total.astype(BF16)[:, 0:96]

    for unless, cp in sent:
        if unless is None:
            cp.wait_send()
        else:
            pl.when(jnp.logical_not(unless))(cp.wait_send)


def shards(tokens, slot_param, slot_outputs, grad_output, grad_slot_in):
    n, f, m = len(NEAR), len(FAR), len(GROUP)
    dma = pltpu.SemaphoreType.DMA
    vmem = pl.BlockSpec(memory_space=pltpu.VMEM)
    slot_in, layer, gtok, gpar, gso = pl.pallas_call(
        kernel,
        out_shape=[
            jax.ShapeDtypeStruct((32, 96), BF16),
            jax.ShapeDtypeStruct((256, 768), BF16),
            jax.ShapeDtypeStruct((256, 768), BF16),
            jax.ShapeDtypeStruct((32, 96), BF16),
            jax.ShapeDtypeStruct((32, 96), BF16),
        ],
        in_specs=[vmem] * 5,
        out_specs=[vmem] * 5,
        scratch_shapes=[
            pltpu.VMEM((3, 32, 128), BF16),
            pltpu.VMEM((3, 256, 1024), BF16),
            pltpu.VMEM((256, 1024), BF16),
            pltpu.VMEM((256, 1024), BF16),
            pltpu.VMEM((3, 256, 256), F32),
            pltpu.VMEM((3, m, 32, 256), F32),
            pltpu.VMEM((3, 32, 256), F32),
            pltpu.VMEM((3, 256, 256), F32),
            pltpu.VMEM((n + 1, 2, 256), F32),
            pltpu.VMEM((n + 1, 2, 256), F32),
            pltpu.VMEM((f + 1, 2, 256), F32),
            pltpu.VMEM((f + 1, 2, 256), F32),
            pltpu.VMEM((256, 256), F32),
            pltpu.VMEM((3, 256, 1024), BF16),
            pltpu.VMEM((3, n, 64, 256), BF16),
            pltpu.VMEM((3, 4, 32, 128), BF16),
            pltpu.VMEM((3, 4, 32, 128), BF16),
            dma((3, 4)), dma((3, 4)),
            dma((3, n)), dma((3, n)),
            dma((3, m)), dma((3, m)),
            dma((3, m)), dma((3, m)),
            dma((2, n)), dma((2, n)),
            dma((2, f)), dma((2, f)),
            dma((3, n)), dma((3, n)),
            dma((3, 4)), dma((3, 4)),
        ],
        compiler_params=pltpu.CompilerParams(
            collective_id=0, has_side_effects=True, vmem_limit_bytes=40 * 1024 * 1024
        ),
        cost_estimate=pl.CostEstimate(flops=10**9, bytes_accessed=2 * 10**6, transcendentals=10**5),
        name="soft_moe",
    )(tokens, slot_param, slot_outputs, grad_output, grad_slot_in)
    return slot_in, layer, gtok, gpar, gso


def solution(mesh):
    by_seq, by_exp = P("seq", "exp"), P("exp", "seq")
    return jax.shard_map(
        shards,
        mesh=mesh,
        in_specs=(by_seq, by_exp, by_exp, by_seq, by_exp),
        out_specs=(by_exp, by_seq, by_seq, by_exp, by_exp),
        check_vma=False,
    )
```

```python
import jax
import jax.numpy as jnp
from jax import lax
from jax.experimental import pallas as pl
from jax.experimental.pallas import tpu as pltpu
from jax.sharding import PartitionSpec as P

MESH = pl.DeviceIdType.MESH
F32 = jnp.float32
BF16 = jnp.bfloat16

NEAR = [(dx, dz) for dz in (2, 1, -1, 0) for dx in (2, 1, 3, 0) if (dx, dz) != (0, 0)]
FAR = [8, 4, -4]
GROUP = [(dy, dc) for dy in (2, 1, 3, 0) for dc in (1, 0) if (dy, dc) != (0, 0)]
N, M, L = len(NEAR), len(GROUP), len(FAR)
PARAM, COTAN, OUTPUT = 0, 1, 2
BACK, SLOT, GPARAM = 0, 1, 2


def rows_by_rows(left, right):
    return lax.dot_general(left, right, (((1,), (1,)), ((), ())), preferred_element_type=F32)


def dot(left, right):
    return jnp.dot(left, right, preferred_element_type=F32)


def kernel(
    tok_hbm, par_hbm, out_hbm, go_hbm, gsi_hbm,
    slot_in_hbm, layer_hbm, gtok_hbm, gpar_hbm, gso_hbm,
    layer_ref, gtok_ref, owned, tok, go, small, blk, inbox, w, tok_t, go_t, part, red, full,
    grp_m, grp_u, st_m, st_u, far_m, far_u, col_stats, comb, from_combine, disp, q, r1, hold, coll,
    in_sem, out_sem, sp_s, sp_r, wf_s, wf_r, ag_s, ag_r, rs_s, rs_r, eg_s, eg_r,
    gm_s, gm_r, nm_s, nm_r, fm_s, fm_r, p1_s, p1_r, p2_s, p2_r,
):
    s, e = lax.axis_index("seq"), lax.axis_index("exp")
    x, z = s // 16, s % 16
    y, c = e // 2, e % 2
    two = 2 - 4 * c

    loads = [
        pltpu.make_async_copy(src, dst, in_sem.at[i])
        for i, (src, dst) in enumerate((
            (par_hbm, small.at[PARAM]), (gsi_hbm, small.at[COTAN]), (out_hbm, small.at[OUTPUT]),
            (tok_hbm, tok), (go_hbm, go),
        ))
    ]
    for load in loads:
        load.start()

    def near_of(dx, dz):
        dz = two if dz == 2 else dz
        return (x + dx) % 4, (z + dz + 16) % 16

    def near_id(dx, dz):
        nx, nz = near_of(dx, dz)
        return (nx * 16 + nz, e)

    def near_source(dx, dz):
        dz = two if dz == 2 else dz
        return (x - dx + 4) % 4, (z - dz + 16) % 16

    def far_id(dz):
        return (x * 16 + (z + dz + 16) % 16, e)

    def group_id(dy, dc):
        return (s, ((y + dy) % 4) * 2 + (c + dc) % 2)

    def block_of(bx, bz):
        row = pl.multiple_of(96 * (4 * (bx % 2) + bz % 4), 32)
        col = pl.multiple_of(128 * (bx // 2), 128)
        return pl.ds(row, 96), pl.ds(col, 128)

    own_block = block_of(x, z)
    is_primary = z // 4 == 2 * c + x % 2
    not_primary = jnp.logical_not(is_primary)
    primary_id = (x * 16 + 8 * c + 4 * (x % 2) + z % 4, e)
    home_id = ((2 * (y // 2) + (z % 8) // 4) * 16 + z, 2 * x + z // 8)
    home_self = (x == y) & is_primary
    place = 2 * (y % 2) + c

    def owner_id(i):
        return (y * 16 + z, 2 * (2 * (x // 2) + i // 2) + i % 2)

    def owner_self(i):
        return (x == y) & (y == 2 * (x // 2) + i // 2) & (c == i % 2)

    barrier = pltpu.get_barrier_semaphore()

    def greet(device):
        pl.semaphore_signal(barrier, inc=1, device_id=device, device_id_type=MESH)

    for dz in FAR:
        greet(far_id(dz))
    pl.when(jnp.logical_not(home_self))(lambda: greet(home_id))
    for i in range(4):
        pl.when(is_primary & jnp.logical_not(owner_self(i)))(lambda i=i: greet(owner_id(i)))
    for o in NEAR:
        nx, nz = near_source(*o)
        greet((nx * 16 + nz, e))
    for o in GROUP:
        greet(group_id(*o))

    for i in range(3):
        loads[i].wait()
    blk[...] = jnp.zeros_like(blk)
    for a in range(3):
        blk[32 * a:32 * a + 32, 0:96] = small[a]
    loads[3].wait()
    tok_t[...] = tok[...].T
    loads[4].wait()
    go_t[...] = go[...].T

    pl.semaphore_wait(
        barrier,
        N + M + L + 1 + 4 * is_primary.astype(jnp.int32) - 2 * home_self.astype(jnp.int32),
    )

    sent = []

    def drain(keep=0):
        while len(sent) > keep:
            wait, when = sent.pop(0)
            if when is None:
                wait()
            else:
                pl.when(when)(wait)

    def copy(src, dst, ss, rs, device=None):
        return pltpu.make_async_remote_copy(
            src_ref=src, dst_ref=dst, send_sem=ss, recv_sem=rs,
            device_id=near_id(1, 0) if device is None else device, device_id_type=MESH,
        )

    def send(copies, whole, ss, rs, when=None):
        def start():
            for src, dst, device in copies:
                copy(src, dst, ss, rs, device).start()

        if when is None:
            start()
        else:
            pl.when(when)(start)
        sent.append((copy(whole, whole, ss, rs).wait_send, when))

    def receive(whole, ss, rs, when=None):
        wait = copy(whole, whole, ss, rs).wait_recv
        if when is None:
            wait()
        else:
            pl.when(when)(wait)

    send([(blk, inbox.at[place], home_id)], blk, sp_s, sp_r.at[place], jnp.logical_not(home_self))

    @pl.when(home_self)
    def _():
        inbox[place] = blk[...]

    @pl.when(is_primary)
    def _():
        for i in range(4):
            receive(inbox.at[i], sp_s, sp_r.at[i], jnp.logical_not(owner_self(i)))

    def pass_on(a):
        spot = w.at[a, *own_block]
        receive(spot, wf_s.at[a], wf_r.at[a], not_primary)
        send([(spot, spot, near_id(*o)) for o in NEAR], r1.at[a], ag_s.at[a], ag_r.at[a])

    for a in (PARAM, COTAN, OUTPUT):
        spot = w.at[a, *own_block]

        @pl.when(is_primary)
        def _():
            rows = jnp.concatenate([inbox[i, 32 * a:32 * a + 32] for i in range(4)], axis=0)
            w[a, *own_block] = rows.astype(F32).T[0:96].astype(BF16)

        send(
            [(spot, spot, far_id(dz)) for dz in FAR], r1.at[a, pl.ds(0, L)], wf_s.at[a], wf_r.at[a], is_primary
        )
        if a != OUTPUT:
            pass_on(a)

    def gathered(a):
        receive(r1.at[a], ag_s.at[a], ag_r.at[a])

    my_tok = pl.multiple_of(32 * e, 32)

    def scatter(a):
        copies = []
        for i, o in enumerate(GROUP):
            device = group_id(*o)
            spot = part.at[a, pl.ds(pl.multiple_of(32 * device[1], 32), 32)]
            copies.append((spot, red.at[a, i], device))
        send(copies, red.at[a], rs_s.at[a], rs_r.at[a])

    def reduced(a):
        total = part[a, pl.ds(my_tok, 32), :]
        receive(red.at[a], rs_s.at[a], rs_r.at[a])
        for i in range(M):
            total = total + red[a, i]
        full[a, pl.ds(my_tok, 32), :] = total
        return total

    def gather(a):
        spot = full.at[a, pl.ds(my_tok, 32)]
        send([(spot, spot, group_id(*o)) for o in GROUP], red.at[a], eg_s.at[a], eg_r.at[a])

    def complete(a):
        receive(red.at[a], eg_s.at[a], eg_r.at[a])

    def spread(buf, ss, rs, ids, t):
        last = buf.shape[0] - 1
        copies = [(buf.at[last], buf.at[i], device) for i, device in enumerate(ids)]
        send(copies, buf.at[pl.ds(0, last)], ss.at[t], rs.at[t])

    def arrived(buf, ss, rs, t):
        receive(buf.at[pl.ds(0, buf.shape[0] - 1)], ss.at[t], rs.at[t])

    def merge(buf):
        count = buf.shape[0]
        top = buf[0, 0:1]
        for i in range(1, count):
            top = jnp.maximum(top, buf[i, 0:1])
        factors = [jnp.exp(buf[i, 0:1] - top) for i in range(count)]
        total = factors[0] * buf[0, 1:2]
        for i in range(1, count):
            total = total + factors[i] * buf[i, 1:2]
        return top, total, factors

    def merge_inner(buf, factors):
        total = factors[0] * buf[0]
        for i in range(1, buf.shape[0]):
            total = total + factors[i] * buf[i]
        return total

    group_ids = [group_id(*o) for o in GROUP]
    near_ids = [near_id(*o) for o in NEAR]
    far_ids = [far_id(dz) for dz in FAR]

    def partial(a, left_t, right):
        for r in range(3):
            q[a, 256 * r:256 * r + 256, :] = dot(left_t[256 * r:256 * r + 256, :], right).astype(BF16)

    def partial_out(a):
        copies = [(q.at[a, *block_of(*near_of(*o))], r1.at[a, i], near_id(*o)) for i, o in enumerate(NEAR)]
        send(copies, r1.at[a], p1_s.at[a], p1_r.at[a])

    gathered(PARAM)
    part[PARAM] = dot(tok[...], w[PARAM])
    scatter(PARAM)
    pass_on(OUTPUT)
    gathered(COTAN)
    part[COTAN] = dot(tok[...], w[COTAN])
    scatter(COTAN)

    own_logits = reduced(PARAM)
    own_max = jnp.max(own_logits, axis=0, keepdims=True)
    own_exp = jnp.exp(own_logits - own_max)
    grp_m[M, 0:1] = own_max
    grp_m[M, 1:2] = jnp.sum(own_exp, axis=0, keepdims=True)
    spread(grp_m, gm_s, gm_r, group_ids, 0)
    gather(PARAM)
    drain(5)

    arrived(grp_m, gm_s, gm_r, 0)
    group_max, group_total, group_factors = merge(grp_m)
    st_m[N, 0:1] = group_max
    st_m[N, 1:2] = group_total
    spread(st_m, nm_s, nm_r, near_ids, 0)

    own_grad = reduced(COTAN)
    grp_u[M] = jnp.sum(own_exp * own_grad, axis=0, keepdims=True)
    spread(grp_u, gm_s, gm_r, group_ids, 1)

    gathered(OUTPUT)
    part[OUTPUT] = dot(go[...], w[OUTPUT])
    scatter(OUTPUT)
    gather(COTAN)

    complete(PARAM)
    logits = full[PARAM]
    weights = jnp.exp(logits - jnp.max(logits, axis=1, keepdims=True))
    comb[...] = weights / jnp.sum(weights, axis=1, keepdims=True)
    partial(BACK, go_t, comb[...].astype(BF16))

    arrived(grp_u, gm_s, gm_r, 1)
    st_u[N] = merge_inner(grp_u, group_factors)
    spread(st_u, nm_s, nm_r, near_ids, 1)

    arrived(st_m, nm_s, nm_r, 0)
    near_max, near_total, near_factors = merge(st_m)
    far_m[L, 0:1] = near_max
    far_m[L, 1:2] = near_total
    spread(far_m, fm_s, fm_r, far_ids, 0)
    partial_out(BACK)

    partial(SLOT, tok_t, jnp.exp(full[PARAM] - group_max).astype(BF16))
    drain(4)

    reduced(OUTPUT)
    gather(OUTPUT)

    arrived(st_u, nm_s, nm_r, 1)
    far_u[L] = merge_inner(st_u, near_factors)
    spread(far_u, fm_s, fm_r, far_ids, 1)
    partial_out(SLOT)

    complete(COTAN)
    complete(OUTPUT)
    combine_full = comb[...]
    grad_combine = full[OUTPUT]
    from_combine[...] = combine_full * (
        grad_combine - jnp.sum(combine_full * grad_combine, axis=1, keepdims=True)
    )

    arrived(far_m, fm_s, fm_r, 0)
    col_max, col_total, far_factors = merge(far_m)
    col_stats[0:1] = col_max
    col_stats[1:2] = col_total
    disp[...] = jnp.exp(full[PARAM] - col_max) / col_total
    drain(2)

    arrived(far_u, fm_s, fm_r, 1)
    inner = merge_inner(far_u, far_factors) / col_total
    grad_logits = (from_combine[...] + disp[...] * (full[COTAN] - inner)).astype(BF16)
    partial(GPARAM, tok_t, grad_logits)
    partial_out(GPARAM)

    stores = [
        pltpu.make_async_copy(src, dst, out_sem.at[i])
        for i, (src, dst) in enumerate((
            (owned.at[BACK], gso_hbm), (owned.at[SLOT], slot_in_hbm), (owned.at[GPARAM], gpar_hbm),
            (layer_ref, layer_hbm), (gtok_ref, gtok_hbm),
        ))
    ]
    layer_ref[...] = rows_by_rows(comb[...].astype(BF16), w[OUTPUT]).astype(BF16)
    stores[3].start()
    gtok_ref[...] = (
        rows_by_rows(disp[...].astype(BF16), w[COTAN]) + rows_by_rows(grad_logits, w[PARAM])
    ).astype(BF16)
    stores[4].start()

    distance = (z // 4 - 2 * c - x % 2 + 4) % 4
    home_z = 8 * c + 4 * (x % 2) + z % 4
    hold[...] = jnp.zeros_like(hold)
    for a in (BACK, SLOT, GPARAM):
        if a == SLOT:
            half = own_block[1]
            scale = [
                jnp.exp(st_m[i, 0:1, half] - col_stats[0:1, half]) / col_stats[1:2, half]
                for i in range(N + 1)
            ]
        total = q[a, *own_block].astype(F32)
        if a == SLOT:
            total = total * scale[N]
        receive(r1.at[a], p1_s.at[a], p1_r.at[a])
        for i in range(N):
            term = r1[a, i].astype(F32)
            total = total + (term * scale[i] if a == SLOT else term)
        hold[a, :, 0:96] = total.T.astype(BF16)
        for i in range(4):
            here = is_primary & owner_self(i)
            owner = (y * 16 + home_z, 2 * (2 * (x // 2) + i // 2) + i % 2)
            part_of = hold.at[a, pl.ds(32 * i, 32)]
            pl.when(jnp.logical_not(here))(
                copy(part_of, coll.at[a, distance], p2_s.at[a], p2_r.at[a, distance], owner).start
            )

            @pl.when(here)
            def _():
                coll[a, 0] = hold[a, 32 * i:32 * i + 32]

        sent.append((copy(coll.at[a, pl.ds(0, 3)], coll.at[a, pl.ds(0, 3)], p2_s.at[a], p2_r.at[a, 0]).wait_send, home_self))
        sent.append((copy(coll.at[a], coll.at[a], p2_s.at[a], p2_r.at[a, 0]).wait_send, jnp.logical_not(home_self)))

    drain(6)
    for a in (BACK, SLOT, GPARAM):
        for g in range(4):
            receive(coll.at[a, g], p2_s.at[a], p2_r.at[a, g], jnp.logical_not(home_self) if g == 0 else None)
        total = coll[a, 0].astype(F32)
        for g in range(1, 4):
            total = total + coll[a, g].astype(F32)
        owned[a] = total.astype(BF16)[:, 0:96]
        stores[a].start()

    for store in stores:
        store.wait()
    drain()


def store_kernel(*refs):
    sources, targets, stages, sem = refs[:5], refs[5:10], refs[10:15], refs[15]
    loads = [pltpu.make_async_copy(a, b, sem.at[0, i]) for i, (a, b) in enumerate(zip(sources, stages))]
    stores = [pltpu.make_async_copy(a, b, sem.at[1, i]) for i, (a, b) in enumerate(zip(stages, targets))]
    for load in loads:
        load.start()
    for load, store in zip(loads, stores):
        load.wait()
        store.start()
    for store in stores:
        store.wait()


def shards(tokens, slot_param, slot_outputs, grad_output, grad_slot_in):
    dma = pltpu.SemaphoreType.DMA
    hbm = pl.BlockSpec(memory_space=pl.ANY)
    out_shape = [
        jax.ShapeDtypeStruct((32, 96), BF16),
        jax.ShapeDtypeStruct((256, 768), BF16),
        jax.ShapeDtypeStruct((256, 768), BF16),
        jax.ShapeDtypeStruct((32, 96), BF16),
        jax.ShapeDtypeStruct((32, 96), BF16),
    ]
    results = pl.pallas_call(
        kernel,
        out_shape=out_shape,
        in_specs=[hbm] * 5,
        out_specs=[hbm] * 5,
        scratch_shapes=[
            pltpu.VMEM((256, 768), BF16),
            pltpu.VMEM((256, 768), BF16),
            pltpu.VMEM((3, 32, 96), BF16),
            pltpu.VMEM((256, 768), BF16),
            pltpu.VMEM((256, 768), BF16),
            pltpu.VMEM((3, 32, 96), BF16),
            pltpu.VMEM((96, 128), BF16),
            pltpu.VMEM((4, 96, 128), BF16),
            pltpu.VMEM((3, 768, 256), BF16),
            pltpu.VMEM((768, 256), BF16),
            pltpu.VMEM((768, 256), BF16),
            pltpu.VMEM((3, 256, 256), F32),
            pltpu.VMEM((3, M, 32, 256), F32),
            pltpu.VMEM((3, 256, 256), F32),
            pltpu.VMEM((M + 1, 2, 256), F32),
            pltpu.VMEM((M + 1, 1, 256), F32),
            pltpu.VMEM((N + 1, 2, 256), F32),
            pltpu.VMEM((N + 1, 1, 256), F32),
            pltpu.VMEM((L + 1, 2, 256), F32),
            pltpu.VMEM((L + 1, 1, 256), F32),
            pltpu.VMEM((2, 256), F32),
            pltpu.VMEM((256, 256), F32),
            pltpu.VMEM((256, 256), F32),
            pltpu.VMEM((256, 256), F32),
            pltpu.VMEM((3, 768, 256), BF16),
            pltpu.VMEM((3, N, 96, 128), BF16),
            pltpu.VMEM((3, 128, 128), BF16),
            pltpu.VMEM((3, 4, 32, 128), BF16),
            dma((5,)), dma((5,)),
            dma, dma((4,)),
            dma((3,)), dma((3,)),
            dma((3,)), dma((3,)),
            dma((3,)), dma((3,)),
            dma((3,)), dma((3,)),
            dma((2,)), dma((2,)),
            dma((2,)), dma((2,)),
            dma((2,)), dma((2,)),
            dma((3,)), dma((3,)),
            dma((3,)), dma((3, 4)),
        ],
        compiler_params=pltpu.CompilerParams(
            collective_id=0, has_side_effects=True, vmem_limit_bytes=60 * 1024 * 1024
        ),
        cost_estimate=pl.CostEstimate(flops=10**9, bytes_accessed=2 * 10**6, transcendentals=10**5),
        name="soft_moe",
    )(tokens, slot_param, slot_outputs, grad_output, grad_slot_in)
    return pl.pallas_call(
        store_kernel,
        out_shape=out_shape,
        in_specs=[hbm] * 5,
        out_specs=[hbm] * 5,
        scratch_shapes=[pltpu.VMEM(o.shape, o.dtype) for o in out_shape] + [dma((2, 5))],
        compiler_params=pltpu.CompilerParams(vmem_limit_bytes=60 * 1024 * 1024),
        name="store_results",
    )(*results)


def solution(mesh):
    by_seq, by_exp = P("seq", "exp"), P("exp", "seq")
    return jax.shard_map(
        shards,
        mesh=mesh,
        in_specs=(by_seq, by_exp, by_exp, by_seq, by_exp),
        out_specs=(by_exp, by_seq, by_seq, by_exp, by_exp),
        check_vma=False,
    )
```

```python
import jax
import jax.numpy as jnp
from jax import lax
from jax.experimental import pallas as pl
from jax.experimental.pallas import tpu as pltpu
from jax.sharding import PartitionSpec as P

MESH = pl.DeviceIdType.MESH
F32 = jnp.float32
BF16 = jnp.bfloat16

NEAR = [(dx, dz) for dz in (2, 1, -1, 0) for dx in (2, 1, 3, 0) if (dx, dz) != (0, 0)]
FAR = [8, 4, -4]
GROUP = [(dy, dc) for dy in (2, 1, 3, 0) for dc in (1, 0) if (dy, dc) != (0, 0)]
N, M, L = len(NEAR), len(GROUP), len(FAR)
PARAM, COTAN, OUTPUT = 0, 1, 2
BACK, SLOT, GPARAM = 0, 1, 2


def rows_by_rows(left, right):
    return lax.dot_general(left, right, (((1,), (1,)), ((), ())), preferred_element_type=F32)


def dot(left, right):
    return jnp.dot(left, right, preferred_element_type=F32)


def kernel(
    tok_hbm, par_hbm, out_hbm, go_hbm, gsi_hbm,
    slot_in_hbm, layer_hbm, gtok_hbm, gpar_hbm, gso_hbm,
    layer_ref, gtok_ref, owned, tok, go, small, blk, inbox, w, tok_t, go_t, part, red, full, part_b, red_b, full_b,
    grp_m, grp_u, st_m, st_u, far_m, far_u, col_stats, comb, from_combine, disp, q, r1, hold, coll,
    in_sem, out_sem, sp_s, sp_r, wf_s, wf_r, ag_s, ag_r, rs_s, rs_r, eg_s, eg_r,
    gm_s, gm_r, nm_s, nm_r, fm_s, fm_r, p1_s, p1_r, p2_s, p2_r,
):
    s, e = lax.axis_index("seq"), lax.axis_index("exp")
    x, z = s // 16, s % 16
    y, c = e // 2, e % 2
    two = 2 - 4 * c

    loads = [
        pltpu.make_async_copy(src, dst, in_sem.at[i])
        for i, (src, dst) in enumerate((
            (par_hbm, small.at[PARAM]), (gsi_hbm, small.at[COTAN]), (out_hbm, small.at[OUTPUT]),
            (tok_hbm, tok), (go_hbm, go),
        ))
    ]
    for load in loads:
        load.start()

    def near_of(dx, dz):
        dz = two if dz == 2 else dz
        return (x + dx) % 4, (z + dz + 16) % 16

    def near_id(dx, dz):
        nx, nz = near_of(dx, dz)
        return (nx * 16 + nz, e)

    def near_source(dx, dz):
        dz = two if dz == 2 else dz
        return (x - dx + 4) % 4, (z - dz + 16) % 16

    def far_id(dz):
        return (x * 16 + (z + dz + 16) % 16, e)

    def group_id(dy, dc):
        return (s, ((y + dy) % 4) * 2 + (c + dc) % 2)

    def block_of(bx, bz):
        row = pl.multiple_of(96 * (4 * (bx % 2) + bz % 4), 32)
        col = pl.multiple_of(128 * (bx // 2), 128)
        return pl.ds(row, 96), pl.ds(col, 128)

    own_block = block_of(x, z)
    is_primary = z // 4 == 2 * c + x % 2
    not_primary = jnp.logical_not(is_primary)
    primary_id = (x * 16 + 8 * c + 4 * (x % 2) + z % 4, e)
    home_id = ((2 * (y // 2) + (z % 8) // 4) * 16 + z, 2 * x + z // 8)
    home_self = (x == y) & is_primary
    place = 2 * (y % 2) + c

    def owner_id(i):
        return (y * 16 + z, 2 * (2 * (x // 2) + i // 2) + i % 2)

    def owner_self(i):
        return (x == y) & (y == 2 * (x // 2) + i // 2) & (c == i % 2)

    barrier = pltpu.get_barrier_semaphore()

    def greet(device):
        pl.semaphore_signal(barrier, inc=1, device_id=device, device_id_type=MESH)

    for dz in FAR:
        greet(far_id(dz))
    pl.when(jnp.logical_not(home_self))(lambda: greet(home_id))
    for i in range(4):
        pl.when(is_primary & jnp.logical_not(owner_self(i)))(lambda i=i: greet(owner_id(i)))
    for o in NEAR:
        nx, nz = near_source(*o)
        greet((nx * 16 + nz, e))
    for o in GROUP:
        greet(group_id(*o))

    for i in range(3):
        loads[i].wait()
    blk[...] = jnp.zeros_like(blk)
    for a in range(3):
        blk[32 * a:32 * a + 32, 0:96] = small[a]
    loads[3].wait()
    tok_t[...] = tok[...].T
    loads[4].wait()
    go_t[...] = go[...].T

    pl.semaphore_wait(
        barrier,
        N + M + L + 1 + 4 * is_primary.astype(jnp.int32) - 2 * home_self.astype(jnp.int32),
    )

    sent = []

    def drain(keep=0):
        while len(sent) > keep:
            wait, when = sent.pop(0)
            if when is None:
                wait()
            else:
                pl.when(when)(wait)

    def copy(src, dst, ss, rs, device=None):
        return pltpu.make_async_remote_copy(
            src_ref=src, dst_ref=dst, send_sem=ss, recv_sem=rs,
            device_id=near_id(1, 0) if device is None else device, device_id_type=MESH,
        )

    def send(copies, whole, ss, rs, when=None):
        def start():
            for src, dst, device in copies:
                copy(src, dst, ss, rs, device).start()

        if when is None:
            start()
        else:
            pl.when(when)(start)
        sent.append((copy(whole, whole, ss, rs).wait_send, when))

    def receive(whole, ss, rs, when=None):
        wait = copy(whole, whole, ss, rs).wait_recv
        if when is None:
            wait()
        else:
            pl.when(when)(wait)

    send([(blk, inbox.at[place], home_id)], blk, sp_s, sp_r.at[place], jnp.logical_not(home_self))

    @pl.when(home_self)
    def _():
        inbox[place] = blk[...]

    @pl.when(is_primary)
    def _():
        for i in range(4):
            receive(inbox.at[i], sp_s, sp_r.at[i], jnp.logical_not(owner_self(i)))

    def pass_on(a):
        spot = w.at[a, *own_block]
        receive(spot, wf_s.at[a], wf_r.at[a], not_primary)
        send([(spot, spot, near_id(*o)) for o in NEAR], r1.at[a], ag_s.at[a], ag_r.at[a])

    for a in (PARAM, COTAN, OUTPUT):
        spot = w.at[a, *own_block]

        @pl.when(is_primary)
        def _():
            rows = jnp.concatenate([inbox[i, 32 * a:32 * a + 32] for i in range(4)], axis=0)
            w[a, *own_block] = rows.astype(F32).T[0:96].astype(BF16)

        send(
            [(spot, spot, far_id(dz)) for dz in FAR], r1.at[a, pl.ds(0, L)], wf_s.at[a], wf_r.at[a], is_primary
        )
        if a != OUTPUT:
            pass_on(a)

    def gathered(a):
        receive(r1.at[a], ag_s.at[a], ag_r.at[a])

    my_tok = pl.multiple_of(32 * e, 32)

    def parts_of(a):
        return part if a == PARAM else part_b.at[a - 1]

    def terms_of(a):
        return red if a == PARAM else red_b.at[a - 1]

    def sums_of(a):
        return full if a == PARAM else full_b.at[a - 1]

    def scatter(a, product):
        parts, terms = parts_of(a), terms_of(a)
        parts[...] = product.astype(parts.dtype)
        copies = []
        for i, o in enumerate(GROUP):
            device = group_id(*o)
            spot = parts.at[pl.ds(pl.multiple_of(32 * device[1], 32), 32)]
            copies.append((spot, terms.at[i], device))
        send(copies, terms, rs_s.at[a], rs_r.at[a])

    def reduced(a):
        parts, terms, sums = parts_of(a), terms_of(a), sums_of(a)
        total = parts[pl.ds(my_tok, 32), :].astype(F32)
        receive(terms, rs_s.at[a], rs_r.at[a])
        for i in range(M):
            total = total + terms[i].astype(F32)
        total = total.astype(sums.dtype)
        sums[pl.ds(my_tok, 32), :] = total
        return total.astype(F32)

    def gather(a):
        spot = sums_of(a).at[pl.ds(my_tok, 32)]
        send([(spot, spot, group_id(*o)) for o in GROUP], terms_of(a), eg_s.at[a], eg_r.at[a])

    def complete(a):
        receive(terms_of(a), eg_s.at[a], eg_r.at[a])

    def spread(buf, ss, rs, ids, t):
        last = buf.shape[0] - 1
        copies = [(buf.at[last], buf.at[i], device) for i, device in enumerate(ids)]
        send(copies, buf.at[pl.ds(0, last)], ss.at[t], rs.at[t])

    def arrived(buf, ss, rs, t):
        receive(buf.at[pl.ds(0, buf.shape[0] - 1)], ss.at[t], rs.at[t])

    def merge(buf):
        count = buf.shape[0]
        top = buf[0, 0:1]
        for i in range(1, count):
            top = jnp.maximum(top, buf[i, 0:1])
        factors = [jnp.exp(buf[i, 0:1] - top) for i in range(count)]
        total = factors[0] * buf[0, 1:2]
        for i in range(1, count):
            total = total + factors[i] * buf[i, 1:2]
        return top, total, factors

    def merge_inner(buf, factors):
        total = factors[0] * buf[0]
        for i in range(1, buf.shape[0]):
            total = total + factors[i] * buf[i]
        return total

    group_ids = [group_id(*o) for o in GROUP]
    near_ids = [near_id(*o) for o in NEAR]
    far_ids = [far_id(dz) for dz in FAR]

    def partial(a, left_t, right):
        for r in range(3):
            q[a, 256 * r:256 * r + 256, :] = dot(left_t[256 * r:256 * r + 256, :], right).astype(BF16)

    def partial_out(a):
        copies = [(q.at[a, *block_of(*near_of(*o))], r1.at[a, i], near_id(*o)) for i, o in enumerate(NEAR)]
        send(copies, r1.at[a], p1_s.at[a], p1_r.at[a])

    gathered(PARAM)
    scatter(PARAM, dot(tok[...], w[PARAM]))
    pass_on(OUTPUT)

    own_logits = reduced(PARAM)
    own_max = jnp.max(own_logits, axis=0, keepdims=True)
    own_exp = jnp.exp(own_logits - own_max)
    grp_m[M, 0:1] = own_max
    grp_m[M, 1:2] = jnp.sum(own_exp, axis=0, keepdims=True)
    spread(grp_m, gm_s, gm_r, group_ids, 0)
    gather(PARAM)

    gathered(COTAN)
    scatter(COTAN, dot(tok[...], w[COTAN]))
    drain(4)

    arrived(grp_m, gm_s, gm_r, 0)
    group_max, group_total, group_factors = merge(grp_m)
    st_m[N, 0:1] = group_max
    st_m[N, 1:2] = group_total
    spread(st_m, nm_s, nm_r, near_ids, 0)

    gathered(OUTPUT)
    scatter(OUTPUT, dot(go[...], w[OUTPUT]))

    complete(PARAM)
    logits = full[...]
    weights = jnp.exp(logits - jnp.max(logits, axis=1, keepdims=True))
    comb[...] = weights / jnp.sum(weights, axis=1, keepdims=True)
    partial(BACK, go_t, comb[...].astype(BF16))

    own_grad = reduced(COTAN)
    grp_u[M] = jnp.sum(own_exp * own_grad, axis=0, keepdims=True)
    spread(grp_u, gm_s, gm_r, group_ids, 1)
    gather(COTAN)
    partial(SLOT, tok_t, jnp.exp(full[...] - group_max).astype(BF16))

    arrived(st_m, nm_s, nm_r, 0)
    near_max, near_total, near_factors = merge(st_m)
    far_m[L, 0:1] = near_max
    far_m[L, 1:2] = near_total
    spread(far_m, fm_s, fm_r, far_ids, 0)
    partial_out(BACK)

    reduced(OUTPUT)
    gather(OUTPUT)

    arrived(grp_u, gm_s, gm_r, 1)
    group_inner = merge_inner(grp_u, group_factors)
    st_u[N] = group_inner
    spread(st_u, nm_s, nm_r, near_ids, 1)
    partial_out(SLOT)
    drain(6)

    complete(COTAN)
    complete(OUTPUT)
    combine_full = comb[...]
    grad_combine = full_b[OUTPUT - 1].astype(F32)
    from_combine[...] = combine_full * (
        grad_combine - jnp.sum(combine_full * grad_combine, axis=1, keepdims=True)
    )

    arrived(st_u, nm_s, nm_r, 1)
    far_u[L] = merge_inner(st_u, near_factors)
    spread(far_u, fm_s, fm_r, far_ids, 1)

    arrived(far_m, fm_s, fm_r, 0)
    col_max, col_total, far_factors = merge(far_m)
    col_stats[0:1] = col_max
    col_stats[1:2] = col_total
    disp[...] = jnp.exp(full[...] - col_max) / col_total

    centre = group_inner / group_total
    grad_dispatch = full_b[COTAN - 1].astype(F32)
    partial(GPARAM, tok_t, (from_combine[...] + disp[...] * (grad_dispatch - centre)).astype(BF16))
    partial_out(GPARAM)
    stores = [
        pltpu.make_async_copy(src, dst, out_sem.at[i])
        for i, (src, dst) in enumerate((
            (owned.at[BACK], gso_hbm), (owned.at[SLOT], slot_in_hbm), (owned.at[GPARAM], gpar_hbm),
            (layer_ref, layer_hbm), (gtok_ref, gtok_hbm),
        ))
    ]
    layer_ref[...] = rows_by_rows(comb[...].astype(BF16), w[OUTPUT]).astype(BF16)
    stores[3].start()

    distance = (z // 4 - 2 * c - x % 2 + 4) % 4
    home_z = 8 * c + 4 * (x % 2) + z % 4
    hold[...] = jnp.zeros_like(hold)
    half = own_block[1]
    for a in (BACK, SLOT, GPARAM):
        if a == SLOT:
            scale = [
                jnp.exp(st_m[i, 0:1, half] - col_stats[0:1, half]) / col_stats[1:2, half]
                for i in range(N + 1)
            ]
        if a == GPARAM:
            arrived(far_u, fm_s, fm_r, 1)
            inner = merge_inner(far_u, far_factors) / col_total
            col_stats[2:3] = inner
            grad_logits = (
                from_combine[...] + disp[...] * (full_b[COTAN - 1].astype(F32) - inner)
            ).astype(BF16)
            gtok_ref[...] = (
                rows_by_rows(disp[...].astype(BF16), w[COTAN]) + rows_by_rows(grad_logits, w[PARAM])
            ).astype(BF16)
            stores[4].start()
        total = q[a, *own_block].astype(F32)
        if a == SLOT:
            total = total * scale[N]
        receive(r1.at[a], p1_s.at[a], p1_r.at[a])
        for i in range(N):
            term = r1[a, i].astype(F32)
            total = total + (term * scale[i] if a == SLOT else term)
        if a == GPARAM:
            for i in range(N + 1):
                shift = (st_u[i, 0:1, half] / st_m[i, 1:2, half] - col_stats[2:3, half]) * scale[i]
                term = r1[SLOT, i] if i < N else q[SLOT, *own_block]
                total = total + term.astype(F32) * shift
        hold[a, :, 0:96] = total.T.astype(BF16)
        for i in range(4):
            here = is_primary & owner_self(i)
            owner = (y * 16 + home_z, 2 * (2 * (x // 2) + i // 2) + i % 2)
            part_of = hold.at[a, pl.ds(32 * i, 32)]
            pl.when(jnp.logical_not(here))(
                copy(part_of, coll.at[a, distance], p2_s.at[a], p2_r.at[a, distance], owner).start
            )

            @pl.when(here)
            def _():
                coll[a, 0] = hold[a, 32 * i:32 * i + 32]

        sent.append((copy(coll.at[a, pl.ds(0, 3)], coll.at[a, pl.ds(0, 3)], p2_s.at[a], p2_r.at[a, 0]).wait_send, home_self))
        sent.append((copy(coll.at[a], coll.at[a], p2_s.at[a], p2_r.at[a, 0]).wait_send, jnp.logical_not(home_self)))

    drain(6)
    for a in (BACK, SLOT, GPARAM):
        for g in range(4):
            receive(coll.at[a, g], p2_s.at[a], p2_r.at[a, g], jnp.logical_not(home_self) if g == 0 else None)
        total = coll[a, 0].astype(F32)
        for g in range(1, 4):
            total = total + coll[a, g].astype(F32)
        owned[a] = total.astype(BF16)[:, 0:96]
        stores[a].start()

    for store in stores:
        store.wait()
    drain()


def store_kernel(*refs):
    sources, targets, stages, sem = refs[:5], refs[5:10], refs[10:15], refs[15]
    loads = [pltpu.make_async_copy(a, b, sem.at[0, i]) for i, (a, b) in enumerate(zip(sources, stages))]
    stores = [pltpu.make_async_copy(a, b, sem.at[1, i]) for i, (a, b) in enumerate(zip(stages, targets))]
    for load in loads:
        load.start()
    for load, store in zip(loads, stores):
        load.wait()
        store.start()
    for store in stores:
        store.wait()


def shards(tokens, slot_param, slot_outputs, grad_output, grad_slot_in):
    dma = pltpu.SemaphoreType.DMA
    hbm = pl.BlockSpec(memory_space=pl.ANY)
    out_shape = [
        jax.ShapeDtypeStruct((32, 96), BF16),
        jax.ShapeDtypeStruct((256, 768), BF16),
        jax.ShapeDtypeStruct((256, 768), BF16),
        jax.ShapeDtypeStruct((32, 96), BF16),
        jax.ShapeDtypeStruct((32, 96), BF16),
    ]
    results = pl.pallas_call(
        kernel,
        out_shape=out_shape,
        in_specs=[hbm] * 5,
        out_specs=[hbm] * 5,
        scratch_shapes=[
            pltpu.VMEM((256, 768), BF16),
            pltpu.VMEM((256, 768), BF16),
            pltpu.VMEM((3, 32, 96), BF16),
            pltpu.VMEM((256, 768), BF16),
            pltpu.VMEM((256, 768), BF16),
            pltpu.VMEM((3, 32, 96), BF16),
            pltpu.VMEM((96, 128), BF16),
            pltpu.VMEM((4, 96, 128), BF16),
            pltpu.VMEM((3, 768, 256), BF16),
            pltpu.VMEM((768, 256), BF16),
            pltpu.VMEM((768, 256), BF16),
            pltpu.VMEM((256, 256), F32),
            pltpu.VMEM((M, 32, 256), F32),
            pltpu.VMEM((256, 256), F32),
            pltpu.VMEM((2, 256, 256), BF16),
            pltpu.VMEM((2, M, 32, 256), BF16),
            pltpu.VMEM((2, 256, 256), BF16),
            pltpu.VMEM((M + 1, 2, 256), F32),
            pltpu.VMEM((M + 1, 1, 256), F32),
            pltpu.VMEM((N + 1, 2, 256), F32),
            pltpu.VMEM((N + 1, 1, 256), F32),
            pltpu.VMEM((L + 1, 2, 256), F32),
            pltpu.VMEM((L + 1, 1, 256), F32),
            pltpu.VMEM((3, 256), F32),
            pltpu.VMEM((256, 256), F32),
            pltpu.VMEM((256, 256), F32),
            pltpu.VMEM((256, 256), F32),
            pltpu.VMEM((3, 768, 256), BF16),
            pltpu.VMEM((3, N, 96, 128), BF16),
            pltpu.VMEM((3, 128, 128), BF16),
            pltpu.VMEM((3, 4, 32, 128), BF16),
            dma((5,)), dma((5,)),
            dma, dma((4,)),
            dma((3,)), dma((3,)),
            dma((3,)), dma((3,)),
            dma((3,)), dma((3,)),
            dma((3,)), dma((3,)),
            dma((2,)), dma((2,)),
            dma((2,)), dma((2,)),
            dma((2,)), dma((2,)),
            dma((3,)), dma((3,)),
            dma((3,)), dma((3, 4)),
        ],
        compiler_params=pltpu.CompilerParams(
            collective_id=0, has_side_effects=True, vmem_limit_bytes=60 * 1024 * 1024
        ),
        cost_estimate=pl.CostEstimate(flops=10**9, bytes_accessed=2 * 10**6, transcendentals=10**5),
        name="soft_moe",
    )(tokens, slot_param, slot_outputs, grad_output, grad_slot_in)
    return pl.pallas_call(
        store_kernel,
        out_shape=out_shape,
        in_specs=[hbm] * 5,
        out_specs=[hbm] * 5,
        scratch_shapes=[pltpu.VMEM(o.shape, o.dtype) for o in out_shape] + [dma((2, 5))],
        compiler_params=pltpu.CompilerParams(vmem_limit_bytes=60 * 1024 * 1024),
        name="store_results",
    )(*results)


def solution(mesh):
    by_seq, by_exp = P("seq", "exp"), P("exp", "seq")
    return jax.shard_map(
        shards,
        mesh=mesh,
        in_specs=(by_seq, by_exp, by_exp, by_seq, by_exp),
        out_specs=(by_exp, by_seq, by_seq, by_exp, by_exp),
        check_vma=False,
    )
```

```python
import jax
import jax.numpy as jnp
from jax import lax
from jax.experimental import pallas as pl
from jax.experimental.pallas import tpu as pltpu
from jax.sharding import PartitionSpec as P

MESH = pl.DeviceIdType.MESH
F32 = jnp.float32
BF16 = jnp.bfloat16

NEAR = [(dx, dz) for dz in (2, 1, -1, 0) for dx in (2, 1, 3, 0) if (dx, dz) != (0, 0)]
FAR = [8, 4, -4]
GROUP = [(dy, dc) for dy in (2, 1, 3, 0) for dc in (1, 0) if (dy, dc) != (0, 0)]
N, M, L = len(NEAR), len(GROUP), len(FAR)
PARAM, COTAN, OUTPUT = 0, 1, 2
BACK, SLOT, GPARAM = 0, 1, 2


def rows_by_rows(left, right):
    return lax.dot_general(left, right, (((1,), (1,)), ((), ())), preferred_element_type=F32)


def dot(left, right):
    return jnp.dot(left, right, preferred_element_type=F32)


def kernel(
    tok_hbm, par_hbm, out_hbm, go_hbm, gsi_hbm,
    slot_in_hbm, layer_hbm, gtok_hbm, gpar_hbm, gso_hbm,
    layer_ref, gtok_ref, owned, tok, go, small, blk, inbox, w, tok_t, go_t, part, red, full, part_b, red_b, full_b,
    grp_m, grp_u, st_m, st_u, far_m, far_u, col_stats, comb, from_combine, disp, q, r1, hold, coll,
    in_sem, out_sem, sp_s, sp_r, wf_s, wf_r, ag_s, ag_r, ah_s, ah_r, rs_s, rs_r, eg_s, eg_r,
    gm_s, gm_r, nm_s, nm_r, fm_s, fm_r, p1_s, p1_r, p2_s, p2_r,
):
    s, e = lax.axis_index("seq"), lax.axis_index("exp")
    x, z = s // 16, s % 16
    y, c = e // 2, e % 2
    two = 2 - 4 * c

    loads = [
        pltpu.make_async_copy(src, dst, in_sem.at[i])
        for i, (src, dst) in enumerate((
            (par_hbm, small.at[PARAM]), (gsi_hbm, small.at[COTAN]), (out_hbm, small.at[OUTPUT]),
            (tok_hbm, tok), (go_hbm, go),
        ))
    ]
    for load in loads:
        load.start()

    def near_of(dx, dz):
        dz = two if dz == 2 else dz
        return (x + dx) % 4, (z + dz + 16) % 16

    def near_id(dx, dz):
        nx, nz = near_of(dx, dz)
        return (nx * 16 + nz, e)

    def near_source(dx, dz):
        dz = two if dz == 2 else dz
        return (x - dx + 4) % 4, (z - dz + 16) % 16

    def far_id(dz):
        return (x * 16 + (z + dz + 16) % 16, e)

    def group_id(dy, dc):
        return (s, ((y + dy) % 4) * 2 + (c + dc) % 2)

    def share_of(bx):
        u = (bx - y + 4) % 4
        return ((u + 1) // 2) % 2, (y // 2 + 1 + u // 2) % 2

    h_own, s_own = share_of(x)

    def block_of(bx, bz):
        h, half = share_of(bx)
        row = pl.multiple_of(96 * (4 * h + bz % 4), 32)
        return pl.ds(row, 96), pl.ds(pl.multiple_of(128 * half, 128), 128)

    own_block = block_of(x, z)
    is_primary = z // 4 == 2 * c + h_own
    not_primary = jnp.logical_not(is_primary)
    h_home = (z % 8) // 4
    same_half = 1 - (y // 2 + x // 2) % 2
    home_x = (x + h_home + same_half * (3 - 2 * h_home)) % 4
    home_id = (home_x * 16 + z, 2 * x + z // 8)
    home_self = (home_x == x) & (x == y) & (c == z // 8)
    place = 2 * (y % 2) + c

    def owner_id(i):
        return (y * 16 + z, 2 * (2 * s_own + i // 2) + i % 2)

    def owner_self(i):
        return (x == y) & (y == 2 * s_own + i // 2) & (c == i % 2)

    barrier = pltpu.get_barrier_semaphore()

    def greet(device):
        pl.semaphore_signal(barrier, inc=1, device_id=device, device_id_type=MESH)

    for dz in FAR:
        greet(far_id(dz))
    pl.when(jnp.logical_not(home_self))(lambda: greet(home_id))
    for i in range(4):
        pl.when(is_primary & jnp.logical_not(owner_self(i)))(lambda i=i: greet(owner_id(i)))
    for o in NEAR:
        nx, nz = near_source(*o)
        greet((nx * 16 + nz, e))
    for o in GROUP:
        greet(group_id(*o))

    for i in range(3):
        loads[i].wait()
    blk[...] = jnp.zeros_like(blk)
    for a in range(3):
        blk[32 * a:32 * a + 32, 0:96] = small[a]
    loads[3].wait()
    tok_t[...] = tok[...].T
    loads[4].wait()
    go_t[...] = go[...].T

    pl.semaphore_wait(
        barrier,
        N + M + L + 1 + 4 * is_primary.astype(jnp.int32) - 2 * home_self.astype(jnp.int32),
    )

    sent = []

    def drain(keep=0):
        while len(sent) > keep:
            wait, when = sent.pop(0)
            if when is None:
                wait()
            else:
                pl.when(when)(wait)

    def copy(src, dst, ss, rs, device=None):
        return pltpu.make_async_remote_copy(
            src_ref=src, dst_ref=dst, send_sem=ss, recv_sem=rs,
            device_id=near_id(1, 0) if device is None else device, device_id_type=MESH,
        )

    def send(copies, whole, ss, rs, when=None):
        def start():
            for src, dst, device in copies:
                copy(src, dst, ss, rs, device).start()

        if when is None:
            start()
        else:
            pl.when(when)(start)
        sent.append((copy(whole, whole, ss, rs).wait_send, when))

    def receive(whole, ss, rs, when=None):
        wait = copy(whole, whole, ss, rs).wait_recv
        if when is None:
            wait()
        else:
            pl.when(when)(wait)

    send([(blk, inbox.at[place], home_id)], blk, sp_s, sp_r.at[place], jnp.logical_not(home_self))

    @pl.when(home_self)
    def _():
        inbox[place] = blk[...]

    @pl.when(is_primary)
    def _():
        for i in range(4):
            receive(inbox.at[i], sp_s, sp_r.at[i], jnp.logical_not(owner_self(i)))

    def first_peers(a):
        if a == PARAM:
            return NEAR
        return [o for o in NEAR if o[a - 1] == 0]

    def pass_on(a):
        spot = w.at[a, *own_block]
        receive(spot, wf_s.at[a], wf_r.at[a], not_primary)
        peers = first_peers(a)
        send([(spot, spot, near_id(*o)) for o in peers], r1.at[a, pl.ds(0, len(peers))], ag_s.at[a], ag_r.at[a])

    def pass_along(a):
        receive(r1.at[a, pl.ds(0, 3)], ag_s.at[a], ag_r.at[a])
        if a == COTAN:
            row, col = pl.multiple_of(384 * h_own, 128), pl.multiple_of(128 * s_own, 128)
            spots = [w.at[a, pl.ds(row, 384), pl.ds(col, 128)]]
        else:
            spots = [w.at[a, pl.ds(pl.multiple_of(96 * (4 * h + z % 4), 32), 96)] for h in (0, 1)]
        peers = [near_id(*o) for o in NEAR if o[2 - a] == 0]
        send([(spot, spot, p) for p in peers for spot in spots], w.at[a, pl.ds(0, 576)], ah_s.at[a - 1], ah_r.at[a - 1])

    for a in (PARAM, COTAN, OUTPUT):
        spot = w.at[a, *own_block]

        @pl.when(is_primary)
        def _():
            rows = jnp.concatenate([inbox[i, 32 * a:32 * a + 32] for i in range(4)], axis=0)
            w[a, *own_block] = rows.astype(F32).T[0:96].astype(BF16)

        send(
            [(spot, spot, far_id(dz)) for dz in FAR], r1.at[a, pl.ds(0, L)], wf_s.at[a], wf_r.at[a], is_primary
        )
        pass_on(a)

    def gathered(a):
        if a == PARAM:
            receive(r1.at[a], ag_s.at[a], ag_r.at[a])
        else:
            receive(w.at[a, pl.ds(0, 576)], ah_s.at[a - 1], ah_r.at[a - 1])

    my_tok = pl.multiple_of(32 * e, 32)

    def parts_of(a):
        return part if a == PARAM else part_b.at[a - 1]

    def terms_of(a):
        return red if a == PARAM else red_b.at[a - 1]

    def sums_of(a):
        return full if a == PARAM else full_b.at[a - 1]

    def scatter(a, product):
        parts, terms = parts_of(a), terms_of(a)
        parts[...] = product.astype(parts.dtype)
        copies = []
        for i, o in enumerate(GROUP):
            device = group_id(*o)
            spot = parts.at[pl.ds(pl.multiple_of(32 * device[1], 32), 32)]
            copies.append((spot, terms.at[i], device))
        send(copies, terms, rs_s.at[a], rs_r.at[a])

    def reduced(a):
        parts, terms, sums = parts_of(a), terms_of(a), sums_of(a)
        total = parts[pl.ds(my_tok, 32), :].astype(F32)
        receive(terms, rs_s.at[a], rs_r.at[a])
        for i in range(M):
            total = total + terms[i].astype(F32)
        total = total.astype(sums.dtype)
        sums[pl.ds(my_tok, 32), :] = total
        return total.astype(F32)

    def gather(a):
        spot = sums_of(a).at[pl.ds(my_tok, 32)]
        send([(spot, spot, group_id(*o)) for o in GROUP], red, eg_s.at[a], eg_r.at[a])

    def complete(a):
        receive(red, eg_s.at[a], eg_r.at[a])

    def spread(buf, ss, rs, ids, t):
        last = buf.shape[0] - 1
        copies = [(buf.at[last], buf.at[i], device) for i, device in enumerate(ids)]
        send(copies, buf.at[pl.ds(0, last)], ss.at[t], rs.at[t])

    def arrived(buf, ss, rs, t):
        receive(buf.at[pl.ds(0, buf.shape[0] - 1)], ss.at[t], rs.at[t])

    def merge(buf):
        count = buf.shape[0]
        top = buf[0, 0:1]
        for i in range(1, count):
            top = jnp.maximum(top, buf[i, 0:1])
        factors = [jnp.exp(buf[i, 0:1] - top) for i in range(count)]
        total = factors[0] * buf[0, 1:2]
        for i in range(1, count):
            total = total + factors[i] * buf[i, 1:2]
        return top, total, factors

    def merge_inner(buf, factors):
        total = factors[0] * buf[0]
        for i in range(1, buf.shape[0]):
            total = total + factors[i] * buf[i]
        return total

    group_ids = [group_id(*o) for o in GROUP]
    near_ids = [near_id(*o) for o in NEAR]
    far_ids = [far_id(dz) for dz in FAR]

    def partial(a, left_t, right):
        for r in range(3):
            q[a, 256 * r:256 * r + 256, :] = dot(left_t[256 * r:256 * r + 256, :], right).astype(BF16)

    def partial_out(a):
        copies = [(q.at[a, *block_of(*near_of(*o))], r1.at[a, i], near_id(*o)) for i, o in enumerate(NEAR)]
        send(copies, r1.at[a], p1_s.at[a], p1_r.at[a])

    gathered(PARAM)
    scatter(PARAM, dot(tok[...], w[PARAM]))
    pass_along(COTAN)
    pass_along(OUTPUT)

    own_logits = reduced(PARAM)
    own_max = jnp.max(own_logits, axis=0, keepdims=True)
    own_exp = jnp.exp(own_logits - own_max)
    grp_m[M, 0:1] = own_max
    grp_m[M, 1:2] = jnp.sum(own_exp, axis=0, keepdims=True)
    spread(grp_m, gm_s, gm_r, group_ids, 0)
    gather(PARAM)

    gathered(COTAN)
    scatter(COTAN, dot(tok[...], w[COTAN]))
    drain(4)

    arrived(grp_m, gm_s, gm_r, 0)
    group_max, group_total, group_factors = merge(grp_m)
    st_m[N, 0:1] = group_max
    st_m[N, 1:2] = group_total
    spread(st_m, nm_s, nm_r, near_ids, 0)

    gathered(OUTPUT)
    scatter(OUTPUT, dot(go[...], w[OUTPUT]))

    complete(PARAM)
    logits = full[...]
    weights = jnp.exp(logits - jnp.max(logits, axis=1, keepdims=True))
    comb[...] = weights / jnp.sum(weights, axis=1, keepdims=True)
    partial(BACK, go_t, comb[...].astype(BF16))
    partial_out(BACK)

    own_grad = reduced(COTAN)
    grp_u[M] = jnp.sum(own_exp * own_grad, axis=0, keepdims=True)
    spread(grp_u, gm_s, gm_r, group_ids, 1)
    gather(COTAN)
    partial(SLOT, tok_t, jnp.exp(full[...] - group_max).astype(BF16))

    arrived(st_m, nm_s, nm_r, 0)
    near_max, near_total, near_factors = merge(st_m)
    far_m[L, 0:1] = near_max
    far_m[L, 1:2] = near_total
    spread(far_m, fm_s, fm_r, far_ids, 0)

    reduced(OUTPUT)
    gather(OUTPUT)

    arrived(grp_u, gm_s, gm_r, 1)
    group_inner = merge_inner(grp_u, group_factors)
    st_u[N] = group_inner
    spread(st_u, nm_s, nm_r, near_ids, 1)
    partial_out(SLOT)
    drain(6)

    complete(COTAN)
    complete(OUTPUT)
    combine_full = comb[...]
    grad_combine = full_b[OUTPUT - 1].astype(F32)
    from_combine[...] = combine_full * (
        grad_combine - jnp.sum(combine_full * grad_combine, axis=1, keepdims=True)
    )

    arrived(far_m, fm_s, fm_r, 0)
    col_max, col_total, far_factors = merge(far_m)
    col_stats[0:1] = col_max
    col_stats[1:2] = col_total
    disp[...] = jnp.exp(full[...] - col_max) / col_total

    centre = group_inner / group_total
    grad_dispatch = full_b[COTAN - 1].astype(F32)
    partial(GPARAM, tok_t, (from_combine[...] + disp[...] * (grad_dispatch - centre)).astype(BF16))
    arrived(st_u, nm_s, nm_r, 1)
    far_u[L] = merge_inner(st_u, near_factors)
    spread(far_u, fm_s, fm_r, far_ids, 1)
    partial_out(GPARAM)
    stores = [
        pltpu.make_async_copy(src, dst, out_sem.at[i])
        for i, (src, dst) in enumerate((
            (owned.at[BACK], gso_hbm), (owned.at[SLOT], slot_in_hbm), (owned.at[GPARAM], gpar_hbm),
            (layer_ref, layer_hbm), (gtok_ref, gtok_hbm),
        ))
    ]
    layer_ref[...] = rows_by_rows(comb[...].astype(BF16), w[OUTPUT]).astype(BF16)
    stores[3].start()

    distance = (z // 4 - 2 * c - h_own + 4) % 4
    home_z = 8 * c + 4 * h_own + z % 4
    hold[...] = jnp.zeros_like(hold)
    half = own_block[1]
    for a in (BACK, SLOT, GPARAM):
        if a == SLOT:
            scale = [
                jnp.exp(st_m[i, 0:1, half] - col_stats[0:1, half]) / col_stats[1:2, half]
                for i in range(N + 1)
            ]
        if a == GPARAM:
            arrived(far_u, fm_s, fm_r, 1)
            inner = merge_inner(far_u, far_factors) / col_total
            col_stats[2:3] = inner
            grad_logits = (
                from_combine[...] + disp[...] * (full_b[COTAN - 1].astype(F32) - inner)
            ).astype(BF16)
            gtok_ref[...] = (
                rows_by_rows(disp[...].astype(BF16), w[COTAN]) + rows_by_rows(grad_logits, w[PARAM])
            ).astype(BF16)
            stores[4].start()
        total = q[a, *own_block].astype(F32)
        if a == SLOT:
            total = total * scale[N]
        if a == GPARAM:
            for i in range(N + 1):
                shift = (st_u[i, 0:1, half] / st_m[i, 1:2, half] - col_stats[2:3, half]) * scale[i]
                term = r1[SLOT, i] if i < N else q[SLOT, *own_block]
                total = total + term.astype(F32) * shift
        receive(r1.at[a], p1_s.at[a], p1_r.at[a])
        for i in range(N):
            term = r1[a, i].astype(F32)
            total = total + (term * scale[i] if a == SLOT else term)
        hold[a, :, 0:96] = total.T.astype(BF16)
        for i in range(4):
            here = is_primary & owner_self(i)
            owner = (y * 16 + home_z, 2 * (2 * s_own + i // 2) + i % 2)
            part_of = hold.at[a, pl.ds(32 * i, 32)]
            pl.when(jnp.logical_not(here))(
                copy(part_of, coll.at[a, distance], p2_s.at[a], p2_r.at[a, distance], owner).start
            )

            @pl.when(here)
            def _():
                coll[a, 0] = hold[a, 32 * i:32 * i + 32]

        sent.append((copy(coll.at[a, pl.ds(0, 3)], coll.at[a, pl.ds(0, 3)], p2_s.at[a], p2_r.at[a, 0]).wait_send, home_self))
        sent.append((copy(coll.at[a], coll.at[a], p2_s.at[a], p2_r.at[a, 0]).wait_send, jnp.logical_not(home_self)))

    drain(6)
    for a in (BACK, SLOT, GPARAM):
        for g in range(4):
            receive(coll.at[a, g], p2_s.at[a], p2_r.at[a, g], jnp.logical_not(home_self) if g == 0 else None)
        total = coll[a, 0].astype(F32)
        for g in range(1, 4):
            total = total + coll[a, g].astype(F32)
        owned[a] = total.astype(BF16)[:, 0:96]
        stores[a].start()

    for store in stores:
        store.wait()
    drain()


def store_kernel(*refs):
    sources, targets, stages, sem = refs[:5], refs[5:10], refs[10:15], refs[15]
    loads = [pltpu.make_async_copy(a, b, sem.at[0, i]) for i, (a, b) in enumerate(zip(sources, stages))]
    stores = [pltpu.make_async_copy(a, b, sem.at[1, i]) for i, (a, b) in enumerate(zip(stages, targets))]
    for load in loads:
        load.start()
    for load, store in zip(loads, stores):
        load.wait()
        store.start()
    for store in stores:
        store.wait()


def shards(tokens, slot_param, slot_outputs, grad_output, grad_slot_in):
    dma = pltpu.SemaphoreType.DMA
    hbm = pl.BlockSpec(memory_space=pl.ANY)
    out_shape = [
        jax.ShapeDtypeStruct((32, 96), BF16),
        jax.ShapeDtypeStruct((256, 768), BF16),
        jax.ShapeDtypeStruct((256, 768), BF16),
        jax.ShapeDtypeStruct((32, 96), BF16),
        jax.ShapeDtypeStruct((32, 96), BF16),
    ]
    results = pl.pallas_call(
        kernel,
        out_shape=out_shape,
        in_specs=[hbm] * 5,
        out_specs=[hbm] * 5,
        scratch_shapes=[
            pltpu.VMEM((256, 768), BF16),
            pltpu.VMEM((256, 768), BF16),
            pltpu.VMEM((3, 32, 96), BF16),
            pltpu.VMEM((256, 768), BF16),
            pltpu.VMEM((256, 768), BF16),
            pltpu.VMEM((3, 32, 96), BF16),
            pltpu.VMEM((96, 128), BF16),
            pltpu.VMEM((4, 96, 128), BF16),
            pltpu.VMEM((3, 768, 256), BF16),
            pltpu.VMEM((768, 256), BF16),
            pltpu.VMEM((768, 256), BF16),
            pltpu.VMEM((256, 256), F32),
            pltpu.VMEM((M, 32, 256), F32),
            pltpu.VMEM((256, 256), F32),
            pltpu.VMEM((2, 256, 256), BF16),
            pltpu.VMEM((2, M, 32, 256), BF16),
            pltpu.VMEM((2, 256, 256), F32),
            pltpu.VMEM((M + 1, 2, 256), F32),
            pltpu.VMEM((M + 1, 1, 256), F32),
            pltpu.VMEM((N + 1, 2, 256), F32),
            pltpu.VMEM((N + 1, 1, 256), F32),
            pltpu.VMEM((L + 1, 2, 256), F32),
            pltpu.VMEM((L + 1, 1, 256), F32),
            pltpu.VMEM((3, 256), F32),
            pltpu.VMEM((256, 256), F32),
            pltpu.VMEM((256, 256), F32),
            pltpu.VMEM((256, 256), F32),
            pltpu.VMEM((3, 768, 256), BF16),
            pltpu.VMEM((3, N, 96, 128), BF16),
            pltpu.VMEM((3, 128, 128), BF16),
            pltpu.VMEM((3, 4, 32, 128), BF16),
            dma((5,)), dma((5,)),
            dma, dma((4,)),
            dma((3,)), dma((3,)),
            dma((3,)), dma((3,)),
            dma((2,)), dma((2,)),
            dma((3,)), dma((3,)),
            dma((3,)), dma((3,)),
            dma((2,)), dma((2,)),
            dma((2,)), dma((2,)),
            dma((2,)), dma((2,)),
            dma((3,)), dma((3,)),
            dma((3,)), dma((3, 4)),
        ],
        compiler_params=pltpu.CompilerParams(
            collective_id=0, has_side_effects=True, vmem_limit_bytes=60 * 1024 * 1024
        ),
        cost_estimate=pl.CostEstimate(flops=10**9, bytes_accessed=2 * 10**6, transcendentals=10**5),
        name="soft_moe",
    )(tokens, slot_param, slot_outputs, grad_output, grad_slot_in)
    return pl.pallas_call(
        store_kernel,
        out_shape=out_shape,
        in_specs=[hbm] * 5,
        out_specs=[hbm] * 5,
        scratch_shapes=[pltpu.VMEM(o.shape, o.dtype) for o in out_shape] + [dma((2, 5))],
        compiler_params=pltpu.CompilerParams(vmem_limit_bytes=60 * 1024 * 1024),
        name="store_results",
    )(*results)


def solution(mesh):
    by_seq, by_exp = P("seq", "exp"), P("exp", "seq")
    return jax.shard_map(
        shards,
        mesh=mesh,
        in_specs=(by_seq, by_exp, by_exp, by_seq, by_exp),
        out_specs=(by_exp, by_seq, by_seq, by_exp, by_exp),
        check_vma=False,
    )
```

```python
import jax
import jax.numpy as jnp
from jax import lax
from jax.experimental import pallas as pl
from jax.experimental.pallas import tpu as pltpu
from jax.sharding import PartitionSpec as P

MESH = pl.DeviceIdType.MESH
F32 = jnp.float32
BF16 = jnp.bfloat16

NEAR = [(dx, dz) for dz in (2, 1, -1, 0) for dx in (2, 1, 3, 0) if (dx, dz) != (0, 0)]
FAR = [8, 4, -4]
GROUP = [(dy, dc) for dy in (2, 1, 3, 0) for dc in (1, 0) if (dy, dc) != (0, 0)]
N, M, L = len(NEAR), len(GROUP), len(FAR)
PLANE = [(dx, dy, dc) for dx in (2, 1, 3, 0) for dy in (2, 1, 3, 0) for dc in (1, 0) if (dx, dy, dc) != (0, 0, 0)]
LINE = [8, 7, -7, 6, -6, 5, -5, 4, -4, 3, -3, 2, -2, 1, -1]
A, B = len(PLANE), len(LINE)
PARAM, COTAN, OUTPUT = 0, 1, 2
BACK, SLOT, GPARAM = 0, 1, 2


def rows_by_rows(left, right):
    return lax.dot_general(left, right, (((1,), (1,)), ((), ())), preferred_element_type=F32)


def dot(left, right):
    return jnp.dot(left, right, preferred_element_type=F32)


def kernel(
    tok_hbm, par_hbm, out_hbm, go_hbm, gsi_hbm,
    slot_in_hbm, layer_hbm, gtok_hbm, gpar_hbm, gso_hbm,
    layer_ref, gtok_ref, owned, tok, go, small, blk, inbox, w, tok_t, go_t, part, red, full, part_b, red_b, full_b,
    pl_m, pl_u, ln_m, ln_u, cen, col_stats, comb, from_combine, disp, expo, q, r1, hold, coll,
    in_sem, out_sem, sp_s, sp_r, wf_s, wf_r, ag_s, ag_r, ah_s, ah_r, rs_s, rs_r, eg_s, eg_r,
    pm_s, pm_r, lm_s, lm_r, cn_s, cn_r, p1_s, p1_r, p2_s, p2_r,
):
    s, e = lax.axis_index("seq"), lax.axis_index("exp")
    x, z = s // 16, s % 16
    y, c = e // 2, e % 2
    two = 2 - 4 * c

    loads = [
        pltpu.make_async_copy(src, dst, in_sem.at[i])
        for i, (src, dst) in enumerate((
            (par_hbm, small.at[PARAM]), (gsi_hbm, small.at[COTAN]), (out_hbm, small.at[OUTPUT]),
            (tok_hbm, tok), (go_hbm, go),
        ))
    ]
    for load in loads:
        load.start()

    def near_of(dx, dz):
        dz = two if dz == 2 else dz
        return (x + dx) % 4, (z + dz + 16) % 16

    def near_id(dx, dz):
        nx, nz = near_of(dx, dz)
        return (nx * 16 + nz, e)

    def near_source(dx, dz):
        dz = two if dz == 2 else dz
        return (x - dx + 4) % 4, (z - dz + 16) % 16

    def far_id(dz):
        return (x * 16 + (z + dz + 16) % 16, e)

    def group_id(dy, dc):
        return (s, ((y + dy) % 4) * 2 + (c + dc) % 2)

    def share_of(bx):
        u = (bx - y + 4) % 4
        return ((u + 1) // 2) % 2, (y // 2 + 1 + u // 2) % 2

    h_own, s_own = share_of(x)

    def block_of(bx, bz):
        h, half = share_of(bx)
        row = pl.multiple_of(96 * (4 * h + bz % 4), 32)
        return pl.ds(row, 96), pl.ds(pl.multiple_of(128 * half, 128), 128)

    own_block = block_of(x, z)
    is_primary = z // 4 == 2 * c + h_own
    not_primary = jnp.logical_not(is_primary)
    h_home = (z % 8) // 4
    same_half = 1 - (y // 2 + x // 2) % 2
    home_x = (x + h_home + same_half * (3 - 2 * h_home)) % 4
    home_id = (home_x * 16 + z, 2 * x + z // 8)
    home_self = (home_x == x) & (x == y) & (c == z // 8)
    place = 2 * (y % 2) + c

    def owner_id(i):
        return (y * 16 + z, 2 * (2 * s_own + i // 2) + i % 2)

    def owner_self(i):
        return (x == y) & (y == 2 * s_own + i // 2) & (c == i % 2)

    barrier = pltpu.get_barrier_semaphore()

    def greet(device):
        pl.semaphore_signal(barrier, inc=1, device_id=device, device_id_type=MESH)

    for dz in FAR:
        greet(far_id(dz))
    pl.when(jnp.logical_not(home_self))(lambda: greet(home_id))
    for i in range(4):
        pl.when(is_primary & jnp.logical_not(owner_self(i)))(lambda i=i: greet(owner_id(i)))
    for o in NEAR:
        nx, nz = near_source(*o)
        greet((nx * 16 + nz, e))
    for o in GROUP:
        greet(group_id(*o))

    for i in range(3):
        loads[i].wait()
    blk[...] = jnp.zeros_like(blk)
    for a in range(3):
        blk[32 * a:32 * a + 32, 0:96] = small[a]
    loads[3].wait()
    tok_t[...] = tok[...].T
    loads[4].wait()
    go_t[...] = go[...].T

    pl.semaphore_wait(
        barrier,
        N + M + L + 1 + 4 * is_primary.astype(jnp.int32) - 2 * home_self.astype(jnp.int32),
    )

    sent = []

    def drain(keep=0):
        while len(sent) > keep:
            wait, when = sent.pop(0)
            if when is None:
                wait()
            else:
                pl.when(when)(wait)

    def copy(src, dst, ss, rs, device=None):
        return pltpu.make_async_remote_copy(
            src_ref=src, dst_ref=dst, send_sem=ss, recv_sem=rs,
            device_id=near_id(1, 0) if device is None else device, device_id_type=MESH,
        )

    def send(copies, whole, ss, rs, when=None):
        def start():
            for src, dst, device in copies:
                copy(src, dst, ss, rs, device).start()

        if when is None:
            start()
        else:
            pl.when(when)(start)
        sent.append((copy(whole, whole, ss, rs).wait_send, when))

    def receive(whole, ss, rs, when=None):
        wait = copy(whole, whole, ss, rs).wait_recv
        if when is None:
            wait()
        else:
            pl.when(when)(wait)

    send([(blk, inbox.at[place], home_id)], blk, sp_s, sp_r.at[place], jnp.logical_not(home_self))

    @pl.when(home_self)
    def _():
        inbox[place] = blk[...]

    @pl.when(is_primary)
    def _():
        for i in range(4):
            receive(inbox.at[i], sp_s, sp_r.at[i], jnp.logical_not(owner_self(i)))

    def first_peers(a):
        if a == PARAM:
            return NEAR
        return [o for o in NEAR if o[a - 1] == 0]

    def pass_on(a):
        spot = w.at[a, *own_block]
        receive(spot, wf_s.at[a], wf_r.at[a], not_primary)
        peers = first_peers(a)
        send([(spot, spot, near_id(*o)) for o in peers], r1.at[a, pl.ds(0, len(peers))], ag_s.at[a], ag_r.at[a])

    def pass_along(a):
        receive(r1.at[a, pl.ds(0, 3)], ag_s.at[a], ag_r.at[a])
        if a == COTAN:
            row, col = pl.multiple_of(384 * h_own, 128), pl.multiple_of(128 * s_own, 128)
            spots = [w.at[a, pl.ds(row, 384), pl.ds(col, 128)]]
        else:
            spots = [w.at[a, pl.ds(pl.multiple_of(96 * (4 * h + z % 4), 32), 96)] for h in (0, 1)]
        peers = [near_id(*o) for o in NEAR if o[2 - a] == 0]
        send([(spot, spot, p) for p in peers for spot in spots], w.at[a, pl.ds(0, 576)], ah_s.at[a - 1], ah_r.at[a - 1])

    for a in (PARAM, COTAN, OUTPUT):
        spot = w.at[a, *own_block]

        @pl.when(is_primary)
        def _():
            rows = jnp.concatenate([inbox[i, 32 * a:32 * a + 32] for i in range(4)], axis=0)
            w[a, *own_block] = rows.astype(F32).T[0:96].astype(BF16)

        send(
            [(spot, spot, far_id(dz)) for dz in FAR], r1.at[a, pl.ds(0, L)], wf_s.at[a], wf_r.at[a], is_primary
        )
        pass_on(a)

    def gathered(a):
        if a == PARAM:
            receive(r1.at[a], ag_s.at[a], ag_r.at[a])
        else:
            receive(w.at[a, pl.ds(0, 576)], ah_s.at[a - 1], ah_r.at[a - 1])

    my_tok = pl.multiple_of(32 * e, 32)

    def parts_of(a):
        return part if a == PARAM else part_b.at[a - 1]

    def terms_of(a):
        return red if a == PARAM else red_b.at[a - 1]

    def sums_of(a):
        return full if a == PARAM else full_b.at[a - 1]

    def scatter(a, product):
        parts, terms = parts_of(a), terms_of(a)
        parts[...] = product.astype(parts.dtype)
        copies = []
        for i, o in enumerate(GROUP):
            device = group_id(*o)
            spot = parts.at[pl.ds(pl.multiple_of(32 * device[1], 32), 32)]
            copies.append((spot, terms.at[i], device))
        send(copies, terms, rs_s.at[a], rs_r.at[a])

    def reduced(a):
        parts, terms, sums = parts_of(a), terms_of(a), sums_of(a)
        total = parts[pl.ds(my_tok, 32), :].astype(F32)
        receive(terms, rs_s.at[a], rs_r.at[a])
        for i in range(M):
            total = total + terms[i].astype(F32)
        total = total.astype(sums.dtype)
        sums[pl.ds(my_tok, 32), :] = total
        return total.astype(F32)

    def gather(a):
        spot = sums_of(a).at[pl.ds(my_tok, 32)]
        send([(spot, spot, group_id(*o)) for o in GROUP], terms_of(a), eg_s.at[a], eg_r.at[a])

    def complete(a):
        receive(terms_of(a), eg_s.at[a], eg_r.at[a])

    def spread(buf, ss, rs, ids, t):
        last = buf.shape[0] - 1
        copies = [(buf.at[last], buf.at[i], device) for i, device in enumerate(ids)]
        send(copies, buf.at[pl.ds(0, last)], ss.at[t], rs.at[t])

    def arrived(buf, ss, rs, t):
        receive(buf.at[pl.ds(0, buf.shape[0] - 1)], ss.at[t], rs.at[t])

    def merge(buf):
        count = buf.shape[0]
        top = buf[0, 0:1]
        for i in range(1, count):
            top = jnp.maximum(top, buf[i, 0:1])
        factors = [jnp.exp(buf[i, 0:1] - top) for i in range(count)]
        total = factors[0] * buf[0, 1:2]
        for i in range(1, count):
            total = total + factors[i] * buf[i, 1:2]
        return top, total, factors

    def merge_inner(buf, factors):
        total = factors[0] * buf[0]
        for i in range(1, buf.shape[0]):
            total = total + factors[i] * buf[i]
        return total

    plane_ids = [
        (((x + dx) % 4) * 16 + z, ((y + dy) % 4) * 2 + (c + dc) % 2) for dx, dy, dc in PLANE
    ]
    line_ids = [far_id(dz) for dz in LINE]
    near_ids = [near_id(*o) for o in NEAR]

    def partial(a, left_t, right):
        for r in range(3):
            q[a, 256 * r:256 * r + 256, :] = dot(left_t[256 * r:256 * r + 256, :], right).astype(BF16)

    def partial_out(a):
        copies = [(q.at[a, *block_of(*near_of(*o))], r1.at[a, i], near_id(*o)) for i, o in enumerate(NEAR)]
        send(copies, r1.at[a], p1_s.at[a], p1_r.at[a])

    gathered(PARAM)
    scatter(PARAM, dot(tok[...], w[PARAM]))
    pass_along(COTAN)
    pass_along(OUTPUT)

    own_logits = reduced(PARAM)
    own_max = jnp.max(own_logits, axis=0, keepdims=True)
    own_exp = jnp.exp(own_logits - own_max)
    pl_m[A, 0:1] = own_max
    pl_m[A, 1:2] = jnp.sum(own_exp, axis=0, keepdims=True)
    spread(pl_m, pm_s, pm_r, plane_ids, 0)
    gather(PARAM)

    gathered(COTAN)
    scatter(COTAN, dot(tok[...], w[COTAN]))
    drain(4)

    arrived(pl_m, pm_s, pm_r, 0)
    plane_max, plane_total, plane_factors = merge(pl_m)
    ln_m[B, 0:1] = plane_max
    ln_m[B, 1:2] = plane_total
    spread(ln_m, lm_s, lm_r, line_ids, 0)

    gathered(OUTPUT)
    scatter(OUTPUT, dot(go[...], w[OUTPUT]))

    complete(PARAM)
    logits = full[...]
    weights = jnp.exp(logits - jnp.max(logits, axis=1, keepdims=True))
    comb[...] = weights / jnp.sum(weights, axis=1, keepdims=True)
    partial(BACK, go_t, comb[...].astype(BF16))
    partial_out(BACK)

    own_grad = reduced(COTAN)
    pl_u[A] = jnp.sum(own_exp * own_grad, axis=0, keepdims=True)
    spread(pl_u, pm_s, pm_r, plane_ids, 1)
    gather(COTAN)
    expo[...] = jnp.exp(full[...] - plane_max)
    partial(SLOT, tok_t, expo[...].astype(BF16))
    partial_out(SLOT)

    reduced(OUTPUT)
    gather(OUTPUT)

    complete(COTAN)
    centre = jnp.sum(expo[...] * full_b[COTAN - 1].astype(F32), axis=0, keepdims=True) / (
        jnp.maximum(jnp.sum(expo[...], axis=0, keepdims=True), 1e-30)
    )
    cen[N] = centre
    spread(cen, cn_s, cn_r, near_ids, 0)

    complete(OUTPUT)
    combine_full = comb[...]
    grad_combine = full_b[OUTPUT - 1].astype(F32)
    from_combine[...] = combine_full * (
        grad_combine - jnp.sum(combine_full * grad_combine, axis=1, keepdims=True)
    )

    arrived(ln_m, lm_s, lm_r, 0)
    col_max, col_total, line_factors = merge(ln_m)
    col_stats[0:1] = col_max
    col_stats[1:2] = col_total
    disp[...] = jnp.exp(full[...] - col_max) / col_total
    grad_dispatch = full_b[COTAN - 1].astype(F32)
    partial(GPARAM, tok_t, (from_combine[...] + disp[...] * (grad_dispatch - centre)).astype(BF16))

    arrived(pl_u, pm_s, pm_r, 1)
    ln_u[B] = merge_inner(pl_u, plane_factors)
    spread(ln_u, lm_s, lm_r, line_ids, 1)
    partial_out(GPARAM)
    drain(6)

    stores = [
        pltpu.make_async_copy(src, dst, out_sem.at[i])
        for i, (src, dst) in enumerate((
            (owned.at[BACK], gso_hbm), (owned.at[SLOT], slot_in_hbm), (owned.at[GPARAM], gpar_hbm),
            (layer_ref, layer_hbm), (gtok_ref, gtok_hbm),
        ))
    ]
    layer_ref[...] = rows_by_rows(comb[...].astype(BF16), w[OUTPUT]).astype(BF16)
    stores[3].start()

    distance = (z // 4 - 2 * c - h_own + 4) % 4
    home_z = 8 * c + 4 * h_own + z % 4
    hold[...] = jnp.zeros_like(hold)
    half = own_block[1]
    for a in (BACK, SLOT, GPARAM):
        if a == GPARAM:
            arrived(ln_u, lm_s, lm_r, 1)
            inner = merge_inner(ln_u, line_factors) / col_total
            col_stats[2:3] = inner
        total = q[a, *own_block].astype(F32)
        receive(r1.at[a], p1_s.at[a], p1_r.at[a])
        if a == SLOT:
            arrived(cen, cn_s, cn_r, 0)
            at_z = {0: B, 1: LINE.index(1), -1: LINE.index(-1), 2: jnp.where(c == 0, LINE.index(2), LINE.index(-2))}
            scale = {
                dz: jnp.exp(ln_m[i, 0:1, half] - col_stats[0:1, half]) / col_stats[1:2, half]
                for dz, i in at_z.items()
            }
            total = total * scale[0]
            centred = total * cen[N, 0:1, half]
            for i, (dx, dz) in enumerate(NEAR):
                term = r1[SLOT, i].astype(F32) * scale[dz]
                total = total + term
                centred = centred + term * cen[i, 0:1, half]
            slot_total = total
        else:
            for i in range(N):
                total = total + r1[a, i].astype(F32)
        if a == GPARAM:
            total = total + centred - slot_total * col_stats[2:3, half]
        hold[a, :, 0:96] = total.T.astype(BF16)
        for i in range(4):
            here = is_primary & owner_self(i)
            owner = (y * 16 + home_z, 2 * (2 * s_own + i // 2) + i % 2)
            part_of = hold.at[a, pl.ds(32 * i, 32)]
            pl.when(jnp.logical_not(here))(
                copy(part_of, coll.at[a, distance], p2_s.at[a], p2_r.at[a, distance], owner).start
            )

            @pl.when(here)
            def _():
                coll[a, 0] = hold[a, 32 * i:32 * i + 32]

        sent.append((copy(coll.at[a, pl.ds(0, 3)], coll.at[a, pl.ds(0, 3)], p2_s.at[a], p2_r.at[a, 0]).wait_send, home_self))
        sent.append((copy(coll.at[a], coll.at[a], p2_s.at[a], p2_r.at[a, 0]).wait_send, jnp.logical_not(home_self)))

    grad_logits = (from_combine[...] + disp[...] * (full_b[COTAN - 1].astype(F32) - col_stats[2:3])).astype(BF16)
    gtok_ref[...] = (
        rows_by_rows(disp[...].astype(BF16), w[COTAN]) + rows_by_rows(grad_logits, w[PARAM])
    ).astype(BF16)
    stores[4].start()
    drain(6)
    for a in (BACK, SLOT, GPARAM):
        for g in range(4):
            receive(coll.at[a, g], p2_s.at[a], p2_r.at[a, g], jnp.logical_not(home_self) if g == 0 else None)
        total = coll[a, 0].astype(F32)
        for g in range(1, 4):
            total = total + coll[a, g].astype(F32)
        owned[a] = total.astype(BF16)[:, 0:96]
        stores[a].start()

    for store in stores:
        store.wait()
    drain()


def store_kernel(*refs):
    sources, targets, stages, sem = refs[:5], refs[5:10], refs[10:15], refs[15]
    loads = [pltpu.make_async_copy(a, b, sem.at[0, i]) for i, (a, b) in enumerate(zip(sources, stages))]
    stores = [pltpu.make_async_copy(a, b, sem.at[1, i]) for i, (a, b) in enumerate(zip(stages, targets))]
    for load in loads:
        load.start()
    for load, store in zip(loads, stores):
        load.wait()
        store.start()
    for store in stores:
        store.wait()


def shards(tokens, slot_param, slot_outputs, grad_output, grad_slot_in):
    dma = pltpu.SemaphoreType.DMA
    hbm = pl.BlockSpec(memory_space=pl.ANY)
    out_shape = [
        jax.ShapeDtypeStruct((32, 96), BF16),
        jax.ShapeDtypeStruct((256, 768), BF16),
        jax.ShapeDtypeStruct((256, 768), BF16),
        jax.ShapeDtypeStruct((32, 96), BF16),
        jax.ShapeDtypeStruct((32, 96), BF16),
    ]
    results = pl.pallas_call(
        kernel,
        out_shape=out_shape,
        in_specs=[hbm] * 5,
        out_specs=[hbm] * 5,
        scratch_shapes=[
            pltpu.VMEM((256, 768), BF16),
            pltpu.VMEM((256, 768), BF16),
            pltpu.VMEM((3, 32, 96), BF16),
            pltpu.VMEM((256, 768), BF16),
            pltpu.VMEM((256, 768), BF16),
            pltpu.VMEM((3, 32, 96), BF16),
            pltpu.VMEM((96, 128), BF16),
            pltpu.VMEM((4, 96, 128), BF16),
            pltpu.VMEM((3, 768, 256), BF16),
            pltpu.VMEM((768, 256), BF16),
            pltpu.VMEM((768, 256), BF16),
            pltpu.VMEM((256, 256), F32),
            pltpu.VMEM((M, 32, 256), F32),
            pltpu.VMEM((256, 256), F32),
            pltpu.VMEM((2, 256, 256), BF16),
            pltpu.VMEM((2, M, 32, 256), BF16),
            pltpu.VMEM((2, 256, 256), BF16),
            pltpu.VMEM((A + 1, 2, 256), F32),
            pltpu.VMEM((A + 1, 1, 256), F32),
            pltpu.VMEM((B + 1, 2, 256), F32),
            pltpu.VMEM((B + 1, 1, 256), F32),
            pltpu.VMEM((N + 1, 1, 256), F32),
            pltpu.VMEM((3, 256), F32),
            pltpu.VMEM((256, 256), F32),
            pltpu.VMEM((256, 256), F32),
            pltpu.VMEM((256, 256), F32),
            pltpu.VMEM((256, 256), F32),
            pltpu.VMEM((3, 768, 256), BF16),
            pltpu.VMEM((3, N, 96, 128), BF16),
            pltpu.VMEM((3, 128, 128), BF16),
            pltpu.VMEM((3, 4, 32, 128), BF16),
            dma((5,)), dma((5,)),
            dma, dma((4,)),
            dma((3,)), dma((3,)),
            dma((3,)), dma((3,)),
            dma((2,)), dma((2,)),
            dma((3,)), dma((3,)),
            dma((3,)), dma((3,)),
            dma((2,)), dma((2,)),
            dma((2,)), dma((2,)),
            dma((1,)), dma((1,)),
            dma((3,)), dma((3,)),
            dma((3,)), dma((3, 4)),
        ],
        compiler_params=pltpu.CompilerParams(
            collective_id=0, has_side_effects=True, vmem_limit_bytes=60 * 1024 * 1024
        ),
        cost_estimate=pl.CostEstimate(flops=10**9, bytes_accessed=2 * 10**6, transcendentals=10**5),
        name="soft_moe",
    )(tokens, slot_param, slot_outputs, grad_output, grad_slot_in)
    return pl.pallas_call(
        store_kernel,
        out_shape=out_shape,
        in_specs=[hbm] * 5,
        out_specs=[hbm] * 5,
        scratch_shapes=[pltpu.VMEM(o.shape, o.dtype) for o in out_shape] + [dma((2, 5))],
        compiler_params=pltpu.CompilerParams(vmem_limit_bytes=60 * 1024 * 1024),
        name="store_results",
    )(*results)


def solution(mesh):
    by_seq, by_exp = P("seq", "exp"), P("exp", "seq")
    return jax.shard_map(
        shards,
        mesh=mesh,
        in_specs=(by_seq, by_exp, by_exp, by_seq, by_exp),
        out_specs=(by_exp, by_seq, by_seq, by_exp, by_exp),
        check_vma=False,
    )
```

```python
import jax
import jax.numpy as jnp
from jax import lax
from jax.experimental import pallas as pl
from jax.experimental.pallas import tpu as pltpu
from jax.sharding import PartitionSpec as P

MESH = pl.DeviceIdType.MESH
F32 = jnp.float32
BF16 = jnp.bfloat16

NEAR = [(dx, dz) for dz in (0, 1, -1, 2) for dx in (1, 3, 2, 0) if (dx, dz) != (0, 0)]
FAR = [8, 4, -4]
GROUP = [(dy, dc) for dy in (2, 1, 3, 0) for dc in (1, 0) if (dy, dc) != (0, 0)]
N, M, L = len(NEAR), len(GROUP), len(FAR)
PLANE = [(dx, dy, dc) for dx in (2, 1, 3, 0) for dy in (2, 1, 3, 0) for dc in (1, 0) if (dx, dy, dc) != (0, 0, 0)]
LINE = [8, 7, -7, 6, -6, 5, -5, 4, -4, 3, -3, 2, -2, 1, -1]
A, B = len(PLANE), len(LINE)
PARAM, COTAN, OUTPUT = 0, 1, 2
BACK, SLOT, GPARAM = 0, 1, 2


def rows_by_rows(left, right):
    return lax.dot_general(left, right, (((1,), (1,)), ((), ())), preferred_element_type=F32)


def dot(left, right):
    return jnp.dot(left, right, preferred_element_type=F32)


def kernel(
    tok_hbm, par_hbm, out_hbm, go_hbm, gsi_hbm,
    slot_in_hbm, layer_hbm, gtok_hbm, gpar_hbm, gso_hbm,
    layer_ref, gtok_ref, owned, tok, go, small, blk, inbox, w, tok_t, go_t, part, red, full, part_b, red_b, full_b,
    pl_m, pl_u, ln_m, ln_u, cen, col_stats, comb, from_combine, disp, expo, q, r1, hold, coll,
    in_sem, out_sem, sp_s, sp_r, wf_s, wf_r, ag_s, ag_r, ah_s, ah_r, rs_s, rs_r, eg_s, eg_r,
    pm_s, pm_r, lm_s, lm_r, cn_s, cn_r, p1_s, p1_r, p2_s, p2_r,
):
    s, e = lax.axis_index("seq"), lax.axis_index("exp")
    x, z = s // 16, s % 16
    y, c = e // 2, e % 2
    two = 2 - 4 * c

    loads = [
        pltpu.make_async_copy(src, dst, in_sem.at[i])
        for i, (src, dst) in enumerate((
            (par_hbm, small.at[PARAM]), (gsi_hbm, small.at[COTAN]), (out_hbm, small.at[OUTPUT]),
            (tok_hbm, tok), (go_hbm, go),
        ))
    ]
    for load in loads:
        load.start()

    def near_of(dx, dz):
        dz = two if dz == 2 else dz
        return (x + dx) % 4, (z + dz + 16) % 16

    def near_id(dx, dz):
        nx, nz = near_of(dx, dz)
        return (nx * 16 + nz, e)

    def near_source(dx, dz):
        dz = two if dz == 2 else dz
        return (x - dx + 4) % 4, (z - dz + 16) % 16

    def far_id(dz):
        return (x * 16 + (z + dz + 16) % 16, e)

    def group_id(dy, dc):
        return (s, ((y + dy) % 4) * 2 + (c + dc) % 2)

    def share_of(bx):
        u = (bx - y + 4) % 4
        return ((u + 1) // 2) % 2, (y // 2 + 1 + u // 2) % 2

    h_own, s_own = share_of(x)

    def block_of(bx, bz):
        h, half = share_of(bx)
        row = pl.multiple_of(96 * (4 * h + bz % 4), 32)
        return pl.ds(row, 96), pl.ds(pl.multiple_of(128 * half, 128), 128)

    own_block = block_of(x, z)
    is_primary = z // 4 == 2 * c + h_own
    not_primary = jnp.logical_not(is_primary)
    h_home = (z % 8) // 4
    same_half = 1 - (y // 2 + x // 2) % 2
    home_x = (x + h_home + same_half * (3 - 2 * h_home)) % 4
    home_id = (home_x * 16 + z, 2 * x + z // 8)
    home_self = (home_x == x) & (x == y) & (c == z // 8)
    place = 2 * (y % 2) + c

    def owner_id(i):
        return (y * 16 + z, 2 * (2 * s_own + i // 2) + i % 2)

    def owner_self(i):
        return (x == y) & (y == 2 * s_own + i // 2) & (c == i % 2)

    barrier = pltpu.get_barrier_semaphore()

    def greet(device):
        pl.semaphore_signal(barrier, inc=1, device_id=device, device_id_type=MESH)

    for dz in FAR:
        greet(far_id(dz))
    pl.when(jnp.logical_not(home_self))(lambda: greet(home_id))
    for i in range(4):
        pl.when(is_primary & jnp.logical_not(owner_self(i)))(lambda i=i: greet(owner_id(i)))
    for o in NEAR:
        nx, nz = near_source(*o)
        greet((nx * 16 + nz, e))
    for o in GROUP:
        greet(group_id(*o))

    for i in range(3):
        loads[i].wait()
    blk[...] = jnp.zeros_like(blk)
    for a in range(3):
        blk[32 * a:32 * a + 32, 0:96] = small[a]
    loads[3].wait()
    tok_t[...] = tok[...].T
    loads[4].wait()
    go_t[...] = go[...].T

    pl.semaphore_wait(
        barrier,
        N + M + L + 1 + 4 * is_primary.astype(jnp.int32) - 2 * home_self.astype(jnp.int32),
    )

    sent = []

    def drain(keep=0):
        while len(sent) > keep:
            wait, when = sent.pop(0)
            if when is None:
                wait()
            else:
                pl.when(when)(wait)

    def copy(src, dst, ss, rs, device=None):
        return pltpu.make_async_remote_copy(
            src_ref=src, dst_ref=dst, send_sem=ss, recv_sem=rs,
            device_id=near_id(1, 0) if device is None else device, device_id_type=MESH,
        )

    def send(copies, whole, ss, rs, when=None):
        def start():
            for src, dst, device in copies:
                copy(src, dst, ss, rs, device).start()

        if when is None:
            start()
        else:
            pl.when(when)(start)
        sent.append((copy(whole, whole, ss, rs).wait_send, when))

    def receive(whole, ss, rs, when=None):
        wait = copy(whole, whole, ss, rs).wait_recv
        if when is None:
            wait()
        else:
            pl.when(when)(wait)

    send([(blk, inbox.at[place], home_id)], blk, sp_s, sp_r.at[place], jnp.logical_not(home_self))

    @pl.when(home_self)
    def _():
        inbox[place] = blk[...]

    @pl.when(is_primary)
    def _():
        for i in range(4):
            receive(inbox.at[i], sp_s, sp_r.at[i], jnp.logical_not(owner_self(i)))

    def first_peers(a):
        if a == PARAM:
            return NEAR
        return [o for o in NEAR if o[a - 1] == 0]

    def pass_on(a):
        spot = w.at[a, *own_block]
        receive(spot, wf_s.at[a], wf_r.at[a], not_primary)
        peers = first_peers(a)
        send([(spot, spot, near_id(*o)) for o in peers], r1.at[a, pl.ds(0, len(peers))], ag_s.at[a], ag_r.at[a])

    def pass_along(a):
        receive(r1.at[a, pl.ds(0, 3)], ag_s.at[a], ag_r.at[a])
        if a == COTAN:
            row, col = pl.multiple_of(384 * h_own, 128), pl.multiple_of(128 * s_own, 128)
            spots = [w.at[a, pl.ds(row, 384), pl.ds(col, 128)]]
        else:
            spots = [w.at[a, pl.ds(pl.multiple_of(96 * (4 * h + z % 4), 32), 96)] for h in (0, 1)]
        peers = [near_id(*o) for o in NEAR if o[2 - a] == 0]
        send([(spot, spot, p) for p in peers for spot in spots], w.at[a, pl.ds(0, 576)], ah_s.at[a - 1], ah_r.at[a - 1])

    for a in (PARAM, COTAN, OUTPUT):
        spot = w.at[a, *own_block]

        @pl.when(is_primary)
        def _():
            rows = jnp.concatenate([inbox[i, 32 * a:32 * a + 32] for i in range(4)], axis=0)
            w[a, *own_block] = rows.astype(F32).T[0:96].astype(BF16)

        send(
            [(spot, spot, far_id(dz)) for dz in FAR], r1.at[a, pl.ds(0, L)], wf_s.at[a], wf_r.at[a], is_primary
        )
        pass_on(a)

    def gathered(a):
        if a == PARAM:
            receive(r1.at[a], ag_s.at[a], ag_r.at[a])
        else:
            receive(w.at[a, pl.ds(0, 576)], ah_s.at[a - 1], ah_r.at[a - 1])

    my_tok = pl.multiple_of(32 * e, 32)

    def parts_of(a):
        return part if a == PARAM else part_b.at[a - 1]

    def terms_of(a):
        return red if a == PARAM else red_b.at[a - 1]

    def sums_of(a):
        return full if a == PARAM else full_b.at[a - 1]

    def scatter(a, product):
        parts, terms = parts_of(a), terms_of(a)
        parts[...] = product.astype(parts.dtype)
        copies = []
        for i, o in enumerate(GROUP):
            device = group_id(*o)
            spot = parts.at[pl.ds(pl.multiple_of(32 * device[1], 32), 32)]
            copies.append((spot, terms.at[i], device))
        send(copies, terms, rs_s.at[a], rs_r.at[a])

    def reduced(a):
        parts, terms, sums = parts_of(a), terms_of(a), sums_of(a)
        total = parts[pl.ds(my_tok, 32), :].astype(F32)
        receive(terms, rs_s.at[a], rs_r.at[a])
        for i in range(M):
            total = total + terms[i].astype(F32)
        total = total.astype(sums.dtype)
        sums[pl.ds(my_tok, 32), :] = total
        return total.astype(F32)

    def gather(a):
        spot = sums_of(a).at[pl.ds(my_tok, 32)]
        send([(spot, spot, group_id(*o)) for o in GROUP], terms_of(a), eg_s.at[a], eg_r.at[a])

    def complete(a):
        receive(terms_of(a), eg_s.at[a], eg_r.at[a])

    def spread(buf, ss, rs, ids, t):
        last = buf.shape[0] - 1
        copies = [(buf.at[last], buf.at[i], device) for i, device in enumerate(ids)]
        send(copies, buf.at[pl.ds(0, last)], ss.at[t], rs.at[t])

    def arrived(buf, ss, rs, t):
        receive(buf.at[pl.ds(0, buf.shape[0] - 1)], ss.at[t], rs.at[t])

    def merge(buf):
        count = buf.shape[0]
        top = buf[0, 0:1]
        for i in range(1, count):
            top = jnp.maximum(top, buf[i, 0:1])
        factors = [jnp.exp(buf[i, 0:1] - top) for i in range(count)]
        total = factors[0] * buf[0, 1:2]
        for i in range(1, count):
            total = total + factors[i] * buf[i, 1:2]
        return top, total, factors

    def merge_inner(buf, factors):
        total = factors[0] * buf[0]
        for i in range(1, buf.shape[0]):
            total = total + factors[i] * buf[i]
        return total

    plane_ids = [
        (((x + dx) % 4) * 16 + z, ((y + dy) % 4) * 2 + (c + dc) % 2) for dx, dy, dc in PLANE
    ]
    line_ids = [far_id(dz) for dz in LINE]
    near_ids = [near_id(*o) for o in NEAR]

    def partial(a, left_t, right):
        for r in range(3):
            q[a, 256 * r:256 * r + 256, :] = dot(left_t[256 * r:256 * r + 256, :], right).astype(BF16)

    def partial_out(a):
        copies = [(q.at[a, *block_of(*near_of(*o))], r1.at[a, i], near_id(*o)) for i, o in enumerate(NEAR)]
        send(copies, r1.at[a], p1_s.at[a], p1_r.at[a])

    gathered(PARAM)
    scatter(PARAM, dot(tok[...], w[PARAM]))
    pass_along(COTAN)
    pass_along(OUTPUT)

    own_logits = reduced(PARAM)
    own_max = jnp.max(own_logits, axis=0, keepdims=True)
    own_exp = jnp.exp(own_logits - own_max)
    pl_m[A, 0:1] = own_max
    pl_m[A, 1:2] = jnp.sum(own_exp, axis=0, keepdims=True)
    spread(pl_m, pm_s, pm_r, plane_ids, 0)
    gather(PARAM)

    gathered(COTAN)
    scatter(COTAN, dot(tok[...], w[COTAN]))
    drain(4)

    arrived(pl_m, pm_s, pm_r, 0)
    plane_max, plane_total, plane_factors = merge(pl_m)
    ln_m[B, 0:1] = plane_max
    ln_m[B, 1:2] = plane_total
    spread(ln_m, lm_s, lm_r, line_ids, 0)

    gathered(OUTPUT)
    scatter(OUTPUT, dot(go[...], w[OUTPUT]))

    complete(PARAM)
    logits = full[...]
    weights = jnp.exp(logits - jnp.max(logits, axis=1, keepdims=True))
    comb[...] = weights / jnp.sum(weights, axis=1, keepdims=True)
    partial(BACK, go_t, comb[...].astype(BF16))
    partial_out(BACK)

    own_grad = reduced(COTAN)
    pl_u[A] = jnp.sum(own_exp * own_grad, axis=0, keepdims=True)
    spread(pl_u, pm_s, pm_r, plane_ids, 1)
    gather(COTAN)
    expo[...] = jnp.exp(full[...] - plane_max)
    partial(SLOT, tok_t, expo[...].astype(BF16))
    partial_out(SLOT)

    reduced(OUTPUT)
    gather(OUTPUT)

    complete(COTAN)
    centre = jnp.sum(expo[...] * full_b[COTAN - 1].astype(F32), axis=0, keepdims=True) / (
        jnp.maximum(jnp.sum(expo[...], axis=0, keepdims=True), 1e-30)
    )
    cen[N] = centre
    spread(cen, cn_s, cn_r, near_ids, 0)

    complete(OUTPUT)
    combine_full = comb[...]
    grad_combine = full_b[OUTPUT - 1].astype(F32)
    from_combine[...] = combine_full * (
        grad_combine - jnp.sum(combine_full * grad_combine, axis=1, keepdims=True)
    )

    arrived(ln_m, lm_s, lm_r, 0)
    col_max, col_total, line_factors = merge(ln_m)
    col_stats[0:1] = col_max
    col_stats[1:2] = col_total
    disp[...] = jnp.exp(full[...] - col_max) / col_total
    grad_dispatch = full_b[COTAN - 1].astype(F32)
    partial(GPARAM, tok_t, (from_combine[...] + disp[...] * (grad_dispatch - centre)).astype(BF16))

    arrived(pl_u, pm_s, pm_r, 1)
    ln_u[B] = merge_inner(pl_u, plane_factors)
    spread(ln_u, lm_s, lm_r, line_ids, 1)
    partial_out(GPARAM)
    drain(6)

    stores = [
        pltpu.make_async_copy(src, dst, out_sem.at[i])
        for i, (src, dst) in enumerate((
            (owned.at[BACK], gso_hbm), (owned.at[SLOT], slot_in_hbm), (owned.at[GPARAM], gpar_hbm),
            (layer_ref, layer_hbm), (gtok_ref, gtok_hbm),
        ))
    ]
    layer_ref[...] = rows_by_rows(comb[...].astype(BF16), w[OUTPUT]).astype(BF16)
    stores[3].start()

    distance = (z // 4 - 2 * c - h_own + 4) % 4
    home_z = 8 * c + 4 * h_own + z % 4
    hold[...] = jnp.zeros_like(hold)
    half = own_block[1]
    for a in (BACK, SLOT, GPARAM):
        if a == GPARAM:
            arrived(ln_u, lm_s, lm_r, 1)
            inner = merge_inner(ln_u, line_factors) / col_total
            col_stats[2:3] = inner
        total = q[a, *own_block].astype(F32)
        receive(r1.at[a], p1_s.at[a], p1_r.at[a])
        if a == SLOT:
            arrived(cen, cn_s, cn_r, 0)
            at_z = {0: B, 1: LINE.index(1), -1: LINE.index(-1), 2: jnp.where(c == 0, LINE.index(2), LINE.index(-2))}
            scale = {
                dz: jnp.exp(ln_m[i, 0:1, half] - col_stats[0:1, half]) / col_stats[1:2, half]
                for dz, i in at_z.items()
            }
            total = total * scale[0]
            centred = total * cen[N, 0:1, half]
            for i, (dx, dz) in enumerate(NEAR):
                term = r1[SLOT, i].astype(F32) * scale[dz]
                total = total + term
                centred = centred + term * cen[i, 0:1, half]
            slot_total = total
        else:
            for i in range(N):
                total = total + r1[a, i].astype(F32)
        if a == GPARAM:
            total = total + centred - slot_total * col_stats[2:3, half]
        hold[a, :, 0:96] = total.T.astype(BF16)
        for i in range(4):
            here = is_primary & owner_self(i)
            owner = (y * 16 + home_z, 2 * (2 * s_own + i // 2) + i % 2)
            part_of = hold.at[a, pl.ds(32 * i, 32)]
            pl.when(jnp.logical_not(here))(
                copy(part_of, coll.at[a, distance], p2_s.at[a], p2_r.at[a, distance], owner).start
            )

            @pl.when(here)
            def _():
                coll[a, 0] = hold[a, 32 * i:32 * i + 32]

        sent.append((copy(coll.at[a, pl.ds(0, 3)], coll.at[a, pl.ds(0, 3)], p2_s.at[a], p2_r.at[a, 0]).wait_send, home_self))
        sent.append((copy(coll.at[a], coll.at[a], p2_s.at[a], p2_r.at[a, 0]).wait_send, jnp.logical_not(home_self)))

    grad_logits = (from_combine[...] + disp[...] * (full_b[COTAN - 1].astype(F32) - col_stats[2:3])).astype(BF16)
    gtok_ref[...] = (
        rows_by_rows(disp[...].astype(BF16), w[COTAN]) + rows_by_rows(grad_logits, w[PARAM])
    ).astype(BF16)
    stores[4].start()
    drain(6)
    for a in (BACK, SLOT, GPARAM):
        for g in range(4):
            receive(coll.at[a, g], p2_s.at[a], p2_r.at[a, g], jnp.logical_not(home_self) if g == 0 else None)
        total = coll[a, 0].astype(F32)
        for g in range(1, 4):
            total = total + coll[a, g].astype(F32)
        owned[a] = total.astype(BF16)[:, 0:96]
        stores[a].start()

    for store in stores:
        store.wait()
    drain()


def store_kernel(*refs):
    sources, targets, stages, sem = refs[:5], refs[5:10], refs[10:15], refs[15]
    loads = [pltpu.make_async_copy(a, b, sem.at[0, i]) for i, (a, b) in enumerate(zip(sources, stages))]
    stores = [pltpu.make_async_copy(a, b, sem.at[1, i]) for i, (a, b) in enumerate(zip(stages, targets))]
    for load in loads:
        load.start()
    for load, store in zip(loads, stores):
        load.wait()
        store.start()
    for store in stores:
        store.wait()


def shards(tokens, slot_param, slot_outputs, grad_output, grad_slot_in):
    dma = pltpu.SemaphoreType.DMA
    hbm = pl.BlockSpec(memory_space=pl.ANY)
    out_shape = [
        jax.ShapeDtypeStruct((32, 96), BF16),
        jax.ShapeDtypeStruct((256, 768), BF16),
        jax.ShapeDtypeStruct((256, 768), BF16),
        jax.ShapeDtypeStruct((32, 96), BF16),
        jax.ShapeDtypeStruct((32, 96), BF16),
    ]
    results = pl.pallas_call(
        kernel,
        out_shape=out_shape,
        in_specs=[hbm] * 5,
        out_specs=[hbm] * 5,
        scratch_shapes=[
            pltpu.VMEM((256, 768), BF16),
            pltpu.VMEM((256, 768), BF16),
            pltpu.VMEM((3, 32, 96), BF16),
            pltpu.VMEM((256, 768), BF16),
            pltpu.VMEM((256, 768), BF16),
            pltpu.VMEM((3, 32, 96), BF16),
            pltpu.VMEM((96, 128), BF16),
            pltpu.VMEM((4, 96, 128), BF16),
            pltpu.VMEM((3, 768, 256), BF16),
            pltpu.VMEM((768, 256), BF16),
            pltpu.VMEM((768, 256), BF16),
            pltpu.VMEM((256, 256), F32),
            pltpu.VMEM((M, 32, 256), F32),
            pltpu.VMEM((256, 256), F32),
            pltpu.VMEM((2, 256, 256), BF16),
            pltpu.VMEM((2, M, 32, 256), BF16),
            pltpu.VMEM((2, 256, 256), BF16),
            pltpu.VMEM((A + 1, 2, 256), F32),
            pltpu.VMEM((A + 1, 1, 256), F32),
            pltpu.VMEM((B + 1, 2, 256), F32),
            pltpu.VMEM((B + 1, 1, 256), F32),
            pltpu.VMEM((N + 1, 1, 256), F32),
            pltpu.VMEM((3, 256), F32),
            pltpu.VMEM((256, 256), F32),
            pltpu.VMEM((256, 256), F32),
            pltpu.VMEM((256, 256), F32),
            pltpu.VMEM((256, 256), F32),
            pltpu.VMEM((3, 768, 256), BF16),
            pltpu.VMEM((3, N, 96, 128), BF16),
            pltpu.VMEM((3, 128, 128), BF16),
            pltpu.VMEM((3, 4, 32, 128), BF16),
            dma((5,)), dma((5,)),
            dma, dma((4,)),
            dma((3,)), dma((3,)),
            dma((3,)), dma((3,)),
            dma((2,)), dma((2,)),
            dma((3,)), dma((3,)),
            dma((3,)), dma((3,)),
            dma((2,)), dma((2,)),
            dma((2,)), dma((2,)),
            dma((1,)), dma((1,)),
            dma((3,)), dma((3,)),
            dma((3,)), dma((3, 4)),
        ],
        compiler_params=pltpu.CompilerParams(
            collective_id=0, has_side_effects=True, vmem_limit_bytes=60 * 1024 * 1024
        ),
        cost_estimate=pl.CostEstimate(flops=10**9, bytes_accessed=2 * 10**6, transcendentals=10**5),
        name="soft_moe",
    )(tokens, slot_param, slot_outputs, grad_output, grad_slot_in)
    return pl.pallas_call(
        store_kernel,
        out_shape=out_shape,
        in_specs=[hbm] * 5,
        out_specs=[hbm] * 5,
        scratch_shapes=[pltpu.VMEM(o.shape, o.dtype) for o in out_shape] + [dma((2, 5))],
        compiler_params=pltpu.CompilerParams(vmem_limit_bytes=60 * 1024 * 1024),
        name="store_results",
    )(*results)


def solution(mesh):
    by_seq, by_exp = P("seq", "exp"), P("exp", "seq")
    return jax.shard_map(
        shards,
        mesh=mesh,
        in_specs=(by_seq, by_exp, by_exp, by_seq, by_exp),
        out_specs=(by_exp, by_seq, by_seq, by_exp, by_exp),
        check_vma=False,
    )
```
